128 devices in a mesh: dp: 16 (over z_lo, x, core), ctx: 8 (over z_hi, y).
Axes of the slice: x: 4, y: 4, z: 4 (z_hi: 2, z_lo: 2; z = z_hi * 2 + z_lo), core: 2. Of those that a mesh axis runs over, the one named last changes fastest.
Arguments:
- query_rows: bfloat16 [262144, 128], P(('dp', 'ctx')), may hold values from -256 to 256
- key_rows: bfloat16 [262144, 128], P(('dp', 'ctx')), may hold values from -64 to 64
- value_rows: bfloat16 [262144, 128], P(('dp', 'ctx')), may hold values from -6 to 6
- doc_lens: int32 [16, 4], P('dp'), may hold values from 1 to 12288, 16384 in all within a row
- dest_group: int32 [1024], P(('dp', 'ctx')), may hold values from 0 to 15, as said below
- block_pos: int32 [1024], P(('dp', 'ctx')), may hold values from 0 to 63, as said below
Outputs:
- attended: bfloat16 [262144, 128], P(('dp', 'ctx'))
The draws below stay inside these ranges and needn't reach their ends.
Inputs may be any that keep to these rules, and one draw needn't show every extreme that they name: `dest_group`: each device sends its 8 blocks to 8 different sequences, and every device receives exactly 8 blocks, each from a different device along dp with the same ctx index. `block_pos`: in each sequence every block position occurs once; a block that arrives at ctx index c holds a position from c * 8 to c * 8 + 7.
All inputs are finite; a program needn't handle non-finite values.
Results may differ from the reference program's by a relative error of at most 0.0065.
Values may be sent and summed in bfloat16 or wider, within the bound.
A program may use at most 64 MiB of HBM per device.

```python
import math
import jax
import jax.numpy as jnp
import numpy as np
from jax import lax

HEAD = 128
BLK = 256
NB = 8
NDOC = 4
SEQ = 16384
TOKENS = 262144
N_DP = 16
N_CTX = 8


def shared_rows(key):
    key_base = jnp.clip(jax.random.normal(jax.random.fold_in(key, 101), (TOKENS, HEAD), jnp.float32), -5.0, 5.0)
    return key_base


def draw_query_rows(key, part):
    key = jax.random.fold_in(key, 5)
    drawn = jnp.clip(jax.random.normal(key, (TOKENS, HEAD), jnp.float32), -5.0, 5.0)
    return drawn.astype(jnp.bfloat16)


def draw_key_rows(key, part):
    key_base = shared_rows(key)
    return key_base.astype(jnp.bfloat16)


def routing(key):
    context_keys = jax.random.split(jax.random.fold_in(key, 201), N_CTX)
    rotation = jax.vmap(lambda subkey: jax.random.permutation(subkey, N_DP))(context_keys)
    order_keys = jax.random.split(jax.random.fold_in(key, 202), N_DP * N_CTX)
    arrival = jax.vmap(lambda subkey: jax.random.permutation(subkey, NB))(order_keys)
    group_index = jnp.arange(N_DP, dtype=jnp.int32)[:, None, None]
    context_index = jnp.arange(N_CTX, dtype=jnp.int32)[None, :, None]
    slot_index = jnp.arange(NB, dtype=jnp.int32)[None, None, :]
    target = (rotation[context_index, group_index] + slot_index) % N_DP
    position = context_index * NB + arrival[target * N_CTX + context_index, slot_index]
    return (target.reshape(-1).astype(jnp.int32), position.reshape(-1).astype(jnp.int32))


def draw_dest_group(key, part):
    target, position = routing(key)
    return target


def draw_block_pos(key, part):
    target, position = routing(key)
    return position


def level_of(key, shape, cuts, smallest, largest):
    factor_of = 1.0
    for axis_at, blocks in cuts:
        heights = jax.random.uniform(jax.random.fold_in(jax.random.fold_in(key, 6), axis_at), (blocks,), jnp.float32, smallest / len(cuts), largest / len(cuts))
        factor_of = factor_of * jnp.repeat(jnp.exp(heights), shape[axis_at] // blocks).reshape((-1,) + (1,) * (len(shape) - 1 - axis_at))
    return factor_of


def profile(number_of, total, most, slope):
    portions = [(1 << 20) // math.isqrt(rank ** slope) + 1 for rank in range(2, number_of + 1)]
    spare, counts = total - most - (number_of - 1), [1] * (number_of - 1)
    while spare > 0:
        movable = [i for i in range(number_of - 1) if counts[i] < most]
        pool, budget = sum([portions[i] for i in movable]), spare
        for i in movable:
            extra = min(most - counts[i], max(1, budget * portions[i] // pool), spare)
            counts[i] = counts[i] + extra
            spare = spare - extra
    return np.array([most] + counts)


def uneven_parts(own_key, number_of, total, reach, slope):
    if number_of == 2:
        one = jax.random.randint(own_key, (), max(1, total - reach), min(reach, total - 1) + 1)
        return jnp.stack([one, total - one])
    sizes = jnp.asarray(profile(number_of, total, reach, slope), jnp.int32)
    couples = (number_of - 1) // 2
    source_of, taker = sizes[1:1 + 2 * couples:2], sizes[2:2 + 2 * couples:2]
    margin = jnp.minimum(source_of - 1, reach - taker)
    passed = jax.random.randint(jax.random.fold_in(own_key, 1), (couples,), 0, 1 << 20) % (margin + 1)
    sizes = sizes.at[1:1 + 2 * couples:2].set(source_of - passed).at[2:2 + 2 * couples:2].set(taker + passed)
    return sizes[jax.random.permutation(jax.random.fold_in(own_key, 2), number_of)]


def noise(key, dims, deviation, bound, cuts=(), kind=jnp.bfloat16):
    array = deviation * jax.random.normal(key, dims, jnp.float32)
    if cuts:
        array = array * level_of(key, dims, cuts, -0.22, 0.18)
    return jnp.clip(array, -bound, bound).astype(kind)


def setup_inputs(seed: int = 0) -> dict:
    key_list = jax.random.split(jax.random.key(seed), 7)
    query_rows = draw_query_rows(jax.random.fold_in(key_list[6], 71), 0)
    key_rows = draw_key_rows(jax.random.fold_in(key_list[6], 71), 0)
    value_rows = noise(key_list[2], (TOKENS, HEAD), 1.0, 6.0, ((0, 128),))
    doc_lens = jax.vmap(lambda own: uneven_parts(own, NDOC, SEQ, 3 * SEQ // 4, 2))(jax.random.split(key_list[3], N_DP)).reshape((N_DP, NDOC)).astype(jnp.int32)
    dest_group = draw_dest_group(jax.random.fold_in(key_list[6], 71), 0)
    block_pos = draw_block_pos(jax.random.fold_in(key_list[6], 71), 0)
    return {"query_rows": query_rows, "key_rows": key_rows, "value_rows": value_rows, "doc_lens": doc_lens, "dest_group": dest_group, "block_pos": block_pos}


masked_score = -1.0e30


def document_of(positions, doc_starts):
    return jnp.sum((positions[:, None] >= doc_starts[None, :]).astype(jnp.int32), axis=1).astype(jnp.int32)


def reference(query_rows, key_rows, value_rows, doc_lens, dest_group, block_pos):
    seq_rows = NB * BLK * N_CTX
    dev_rows = NB * BLK
    canon_index = (dest_group * (NB * N_CTX) + block_pos).astype(jnp.int32)

    def arrange(source):
        blocks = source.reshape(NB * N_CTX * N_DP, BLK, HEAD)
        placed = jnp.zeros_like(blocks).at[canon_index].set(blocks)
        return placed.reshape(N_DP, seq_rows, HEAD)

    seq_queries = arrange(query_rows)
    seq_keys = arrange(key_rows)
    seq_values = arrange(value_rows)
    lengths = doc_lens.astype(jnp.int32)
    doc_starts = (jnp.cumsum(lengths, axis=1) - lengths).astype(jnp.int32)
    positions = jnp.arange(seq_rows, dtype=jnp.int32)
    score_scale = 1.0 / (HEAD ** 0.5)
    pieces = []
    for segment in range(N_CTX):
        row_lower = segment * dev_rows
        row_upper = row_lower + dev_rows

        def attend(operands):
            seq_query, seq_key, seq_value, starts_row = operands
            query_pos = positions[row_lower:row_upper]
            key_pos = positions[:row_upper]
            query_doc = document_of(query_pos, starts_row)
            key_doc = document_of(key_pos, starts_row)
            scores = jnp.dot(seq_query[row_lower:row_upper], seq_key[:row_upper].T, preferred_element_type=jnp.float32) * score_scale
            allowed = (key_doc[None, :] == query_doc[:, None]) & (key_pos[None, :] <= query_pos[:, None])
            scores = jnp.where(allowed, scores, masked_score)
            row_peak = jnp.max(scores, axis=1)
            weights = jnp.where(allowed, jnp.exp(scores - row_peak[:, None]), 0.0)
            weight_sum = jnp.sum(weights, axis=1)
            context = jnp.dot(weights.astype(jnp.bfloat16), seq_value[:row_upper], preferred_element_type=jnp.float32)
            return (context / weight_sum[:, None]).astype(jnp.bfloat16)

        pieces.append(lax.map(attend, (seq_queries, seq_keys, seq_values, doc_starts)))
    context = jnp.concatenate(pieces, axis=1)
    blocks = context.reshape(NB * N_CTX * N_DP, BLK, HEAD)
    return blocks[canon_index].reshape(NB * BLK * N_CTX * N_DP, HEAD)
```

```python
import functools
import math

import jax
import jax.numpy as jnp
from jax import lax
from jax.experimental import pallas as pl
from jax.experimental.pallas import tpu as pltpu
from jax.sharding import PartitionSpec as P

HEAD = 128
BLK = 256
NB = 8
HALF = BLK // 2
RING = 4
GROUPS = 16
PARTS = 2
SEG = NB * BLK
UNIT = NB * HALF
EXP_SCALE = math.log2(math.e) / math.sqrt(HEAD)
FAR = -(2.0**40)
EMPTY = -1e30
MESH = pl.DeviceIdType.MESH
NT = (((1,), (1,)), ((), ()))


def widened(left, right):
    return jnp.concatenate([left, right], axis=1)


def attend_tiles(tiles, query_of, key_of, value_of, mask_of, peak_ref, acc_ref):
    def scores_of(tile):
        rows, keys = tile
        found = lax.dot_general(
            query_of(rows), key_of(keys), NT, preferred_element_type=jnp.float32
        )
        return found if mask_of is None else jnp.where(mask_of(rows, keys), found, FAR)

    scores = scores_of(tiles[0])
    for at, (rows, keys) in enumerate(tiles):
        following = scores_of(tiles[at + 1]) if at + 1 < len(tiles) else None
        old_peak = peak_ref[rows, :]
        peak = jnp.maximum(old_peak, jnp.max(scores, axis=1, keepdims=True))
        factor = jnp.exp2((old_peak - peak) * EXP_SCALE)
        weights = jnp.exp2((scores - peak[:, :1]) * EXP_SCALE).astype(jnp.bfloat16)
        added = jnp.dot(weights, value_of(keys), preferred_element_type=jnp.float32)
        acc_ref[rows, :] = acc_ref[rows, :] * widened(factor, factor) + added
        peak_ref[rows, :] = peak
        scores = following


def kernel(
    q_ref, k_ref, v_ref, len_ref, group_ref, pos_ref, out_ref,
    q_send, q_recv, kv_send, kv_recv_first, kv_recv_second, kv_all, key_doc, query_doc, queries,
    rank_send, rank_recv, krank_recv, rank_smem, krank_smem, doc_own, doc_recv,
    peak, acc, result, back_send, back_recv,
    q_ssem, q_rsem, m_ssem, m_rsem, km_ssem, km_rsem, kv_ssem, kv_rsem,
    ring_ssem, ring_rsem, core_ssem, core_rsem, doc_ssem, doc_rsem,
    back_ssem, back_rsem, local_sem,
):
    dp = lax.axis_index("dp")
    ctx = lax.axis_index("ctx")
    z_lo, x, core = dp // 8, (dp // 2) % 4, dp % 2
    z_hi, y = ctx // RING, ctx % RING
    mirror = 3 - y
    my_seq = z_lo * 8 + x * 2 + z_hi
    own_seg = core * RING + y
    kv_recv = (kv_recv_first, kv_recv_second)
    query_y = y + z_hi * (mirror - y)
    stays = core == z_hi

    def device(z_lo_, x_, core_, z_hi_, y_):
        return (z_lo_ * 8 + x_ * 2 + core_, z_hi_ * RING + y_)

    up = device(z_lo, x, core, z_hi, (y + 1) % RING)
    down = device(z_lo, x, core, z_hi, (y + 3) % RING)
    twin = device(z_lo, x, 1 - core, z_hi, y)

    def remote(src, dst, ssem, rsem, target):
        return pltpu.make_async_remote_copy(
            src_ref=src, dst_ref=dst, send_sem=ssem, recv_sem=rsem,
            device_id=target, device_id_type=MESH,
        )

    def await_bytes(ref, sem):
        pltpu.make_async_copy(ref, ref, sem).wait()

    barrier = pltpu.get_barrier_semaphore()

    def greet(at, unused):
        peer = ((z_lo + at % 2) % 2, (x + (at // 2) % 4) % 4, (core + (at // 8) % 2) % 2, (z_hi + at // 16) % 2)

        @pl.when(at > 0)
        def _():
            pl.semaphore_signal(barrier, inc=1, device_id=device(*peer, y), device_id_type=MESH)

        pl.semaphore_signal(barrier, inc=1, device_id=device(*peer, mirror), device_id_type=MESH)
        return unused

    lax.fori_loop(0, 32, greet, 0)
    for neighbour in (up, down):
        pl.semaphore_signal(barrier, inc=1, device_id=neighbour, device_id_type=MESH)

    lane = lax.broadcasted_iota(jnp.int32, (1, HEAD), 1)
    begin = jnp.zeros((1, HEAD), jnp.int32)
    until = jnp.full((1, HEAD), 1 << 20, jnp.int32)
    total = jnp.int32(0)
    for document in range(4):
        begin = jnp.where(lane == document, total, begin)
        total = total + len_ref[0, document]
        until = jnp.where(lane == document, total, until)
    doc_own[0] = begin
    doc_own[1] = until

    def arrival(seq):
        slot, rank = jnp.int32(0), jnp.int32(-1)
        for block in range(NB):
            hit = group_ref[block] == seq
            slot = jnp.where(hit, block, slot)
            rank = jnp.where(hit, pos_ref[block] % NB, rank)
        return slot, rank

    def target_of(at):
        return (z_lo + at % 2) % 2, (x + at // 4) % 4, (z_hi + (at // 2) % 2) % 2

    def stage(at, unused):
        z_lo_, x_, seq_core = target_of(at)
        slot, rank = arrival(z_lo_ * 8 + x_ * 2 + seq_core)
        rank_send[at] = jnp.full((1, HEAD), rank, jnp.int32)
        block = q_ref[slot]
        q_send[at, 0] = block[:HALF]
        q_send[at, 1] = block[HALF:]
        keys, values = k_ref[slot], v_ref[slot]
        for part in range(PARTS):
            kv_send[part, at, 0] = keys[part * HALF:(part + 1) * HALF]
            kv_send[part, at, 1] = values[part * HALF:(part + 1) * HALF]
        return unused

    lax.fori_loop(0, GROUPS, stage, 0)
    pl.semaphore_wait(barrier, 65)

    remote(doc_own, doc_recv, doc_ssem, doc_rsem, twin).start()

    def send_ranks(at, unused):
        z_lo_, x_, seq_core = target_of(at)
        for other in range(2):
            half = (core + other) % 2
            here = (at + other == 0) & (query_y == y)

            @pl.when(here)
            def _():
                pltpu.make_async_copy(rank_send.at[at], rank_recv.at[z_hi, dp], m_rsem).start()

            @pl.when(jnp.logical_not(here))
            def _():
                remote(
                    rank_send.at[at], rank_recv.at[z_hi, dp], m_ssem, m_rsem,
                    device(z_lo_, x_, half, seq_core, query_y),
                ).start()

        here = (at == 0) & stays

        @pl.when(here)
        def _():
            pltpu.make_async_copy(rank_send.at[at], krank_recv.at[dp], km_rsem).start()

        @pl.when(jnp.logical_not(here))
        def _():
            remote(
                rank_send.at[at], krank_recv.at[dp], km_ssem, km_rsem, device(z_lo_, x_, z_hi, seq_core, y)
            ).start()

        return unused

    lax.fori_loop(0, GROUPS, send_ranks, 0)

    def send_queries(at, unused):
        z_lo_, x_, seq_core = target_of(at)
        for other in range(2):
            half = (core + other) % 2
            here = (at + other == 0) & (query_y == y)

            @pl.when(here)
            def _():
                pltpu.make_async_copy(q_send.at[at, half], q_recv.at[z_hi, dp], q_rsem).start()

            @pl.when(jnp.logical_not(here))
            def _():
                remote(
                    q_send.at[at, half], q_recv.at[z_hi, dp], q_ssem, q_rsem,
                    device(z_lo_, x_, half, seq_core, query_y),
                ).start()

        return unused

    def send_keys(part):
        def send(at, unused):
            z_lo_, x_, seq_core = target_of(at)
            here = (at == 0) & stays

            @pl.when(here)
            def _():
                pltpu.make_async_copy(kv_send.at[part, at], kv_recv[part].at[dp], kv_rsem.at[part]).start()

            @pl.when(jnp.logical_not(here))
            def _():
                remote(
                    kv_send.at[part, at], kv_recv[part].at[dp], kv_ssem.at[part], kv_rsem.at[part],
                    device(z_lo_, x_, z_hi, seq_core, y),
                ).start()

            return unused

        lax.fori_loop(0, GROUPS, send, 0)

    lax.fori_loop(0, GROUPS, send_queries, 0)
    send_keys(0)
    send_keys(1)

    remote(doc_own, doc_recv, doc_ssem, doc_rsem, twin).wait()
    begin = jnp.where(stays, doc_own[0], doc_recv[0])
    until = jnp.where(stays, doc_own[1], doc_recv[1])
    row = lax.broadcasted_iota(jnp.int32, (HALF, HEAD), 0)
    lanes = lax.broadcasted_iota(jnp.int32, (HALF, HEAD), 1)

    def mark_keys(at, unused):
        part, block = at // (2 * RING * NB), at % (2 * RING * NB)
        place = row + (block * BLK + part * HALF)
        inside = (place >= begin) & (place < until)
        start = pl.multiple_of((block % NB) * HALF, HALF)
        key_doc[part, block // NB, pl.ds(start, HALF), :] = jnp.where(inside, 0.0, FAR).astype(jnp.bfloat16)
        return unused

    lax.fori_loop(0, PARTS * 2 * RING * NB, mark_keys, 0)

    def query_seg(group):
        return y + group * (RING + mirror - y)

    def mark_queries(at, unused):
        group, block = at // NB, at % NB
        place = row + (query_seg(group) * SEG + block * BLK + core * HALF)
        inside = (place >= begin) & (place < until) & (lanes < 4)
        start = pl.multiple_of(block * HALF, HALF)
        query_doc[group, pl.ds(start, HALF), :] = jnp.where(inside, 1.0, 0.0).astype(jnp.bfloat16)
        return unused

    lax.fori_loop(0, 2 * NB, mark_queries, 0)

    def clear(at, unused):
        start = pl.multiple_of(at * HALF, HALF)
        for group in range(2):
            peak[group, pl.ds(start, HALF), :] = jnp.full((HALF, HEAD), EMPTY, jnp.float32)
            acc[group, pl.ds(start, HALF), :] = jnp.zeros((HALF, 2 * HEAD), jnp.float32)
        return unused

    lax.fori_loop(0, NB, clear, 0)

    await_bytes(rank_recv, m_rsem)
    await_bytes(krank_recv, km_rsem)
    ranks_in = pltpu.make_async_copy(rank_recv, rank_smem, local_sem.at[0])
    kranks_in = pltpu.make_async_copy(krank_recv, krank_smem, local_sem.at[1])
    ranks_in.start()
    kranks_in.start()
    ranks_in.wait()
    kranks_in.wait()

    def place_queries(at, unused):
        start = pl.multiple_of(at * HALF, HALF)
        for group in range(2):
            source = jnp.int32(0)
            for sender in range(GROUPS):
                source = jnp.where(rank_smem[group, sender, 0, 0] == at, sender, source)
            queries[group, pl.ds(start, HALF), :] = q_recv[group, source]
        return unused

    def place_keys(part):
        def place(at, unused):
            start = pl.multiple_of(at * HALF, HALF)
            source = jnp.int32(0)
            for sender in range(GROUPS):
                source = jnp.where(krank_smem[sender, 0, 0] == at, sender, source)
            for which in range(2):
                kv_all[part, own_seg, which, pl.ds(start, HALF), :] = kv_recv[part][source, which]
            return unused

        lax.fori_loop(0, NB, place, 0)

    def seg_at(kind, shift):
        return kind * RING + (y + shift) % RING

    def ring_copy(part, which):
        if which == 0:
            here, target = kv_all.at[part, own_seg], up
        elif which == 1:
            here, target = kv_all.at[part, own_seg], down
        elif which == 2:
            here, target = kv_all.at[part, seg_at(core, 3), 0], up
        else:
            here, target = kv_all.at[part, seg_at(core, 1), 1], down
        return remote(here, here, ring_ssem.at[part, which], ring_rsem.at[part, which], target)

    def ring_arrived(part, which):
        if which == 0:
            there = kv_all.at[part, seg_at(core, 3)]
        elif which == 1:
            there = kv_all.at[part, seg_at(core, 1)]
        elif which == 2:
            there = kv_all.at[part, seg_at(core, 2), 0]
        else:
            there = kv_all.at[part, seg_at(core, 2), 1]
        await_bytes(there, ring_rsem.at[part, which])

    shifts = (0, 3, 1, 2)

    def core_copy(part, which):
        here = kv_all.at[part, seg_at(core, shifts[which])]
        return remote(here, here, core_ssem.at[part, which], core_rsem.at[part, which], twin)

    def core_arrived(part, which):
        await_bytes(kv_all.at[part, seg_at(1 - core, shifts[which])], core_rsem.at[part, which])

    def start_part(part):
        await_bytes(kv_recv[part], kv_rsem.at[part])
        place_keys(part)
        ring_copy(part, 0).start()
        ring_copy(part, 1).start()
        core_copy(part, 0).start()

    def next_segment(part, step):
        @pl.when(step == 1)
        def _():
            core_arrived(part, 0)

        @pl.when(step == 2)
        def _():
            ring_arrived(part, 0)
            ring_copy(part, 2).start()
            core_copy(part, 1).start()
            ring_arrived(part, 1)
            ring_copy(part, 3).start()
            core_copy(part, 2).start()

        @pl.when(step == 4)
        def _():
            core_arrived(part, 1)

        @pl.when(step == 5)
        def _():
            core_arrived(part, 2)

        @pl.when(step == 6)
        def _():
            ring_arrived(part, 2)
            ring_arrived(part, 3)
            core_copy(part, 3).start()

        @pl.when(step == 7)
        def _():
            core_arrived(part, 3)

    def unit(part, seg, group, tiles, masked):
        query_row = lax.broadcasted_iota(jnp.int32, (UNIT // 2, 1), 0)

        def mask_of(rows, keys):
            at = query_row + rows.start
            query_place = (at // HALF) * BLK + core * HALF + at % HALF
            key = lax.broadcasted_iota(jnp.int32, (1, keys.size), 1) + keys.start
            key_place = (key // HALF) * BLK + part * HALF + key % HALF
            return key_place <= query_place

        attend_tiles(
            tiles,
            lambda rows: widened(queries[group, rows, :], query_doc[group, rows, :]),
            lambda keys: widened(kv_all[part, seg, 0, keys, :], key_doc[part, seg, keys, :]),
            lambda keys: widened(kv_all[part, seg, 1, keys, :], jnp.ones((keys.size, HEAD), jnp.bfloat16)),
            mask_of if masked else None,
            peak.at[group],
            acc.at[group],
        )

    low, high, whole = pl.ds(0, UNIT // 2), pl.ds(UNIT // 2, UNIT // 2), pl.ds(0, UNIT)

    def visit(at, unused):
        part, step = at // 8, at % 8
        for known in range(PARTS):
            @pl.when(part == known)
            def _():
                next_segment(known, step)

        @pl.when(at == 4)
        def _():
            start_part(1)

        other = jnp.where((step == 1) | (step == 4) | (step == 5) | (step == 7), 1, 0)
        shift = jnp.where((step == 2) | (step == 4), 3, jnp.where((step == 3) | (step == 5), 1, jnp.where(step >= 6, 2, 0)))
        kind = (core + other) % 2
        seg = kind * RING + (y + shift) % RING

        def per_group(group, carried):
            wanted = query_seg(group)

            @pl.when(seg < wanted)
            def _():
                unit(part, seg, group, [(low, whole), (high, whole)], False)

            @pl.when(seg == wanted)
            def _():
                unit(part, seg, group, [(low, low), (high, whole)], True)

            return carried

        return lax.fori_loop(0, 2, per_group, unused)

    await_bytes(q_recv, q_rsem)
    lax.fori_loop(0, NB, place_queries, 0)
    start_part(0)
    lax.fori_loop(0, 8 * PARTS, visit, 0)

    def finish(at, unused):
        start = pl.multiple_of(at * HALF, HALF)
        for group in range(2):
            both = acc[group, pl.ds(start, HALF), :]
            result[group, at] = (both[:, :HEAD] / both[:, HEAD:]).astype(jnp.bfloat16)
        return unused

    lax.fori_loop(0, NB, finish, 0)

    def send_back(at, unused):
        z_lo_, x_, core_ = target_of(at)
        core_ = (core + (at // 2) % 2) % 2
        sender = z_lo_ * 8 + x_ * 2 + core_
        for other in range(2):
            group = (z_hi + other) % 2
            source_y = y + group * (mirror - y)
            rank = jnp.maximum(rank_smem[group, sender, 0, 0], 0)
            back_send[at, other] = result[group, rank]
            here = (at + other == 0) & (source_y == y)

            @pl.when(here)
            def _():
                pltpu.make_async_copy(back_send.at[at, other], back_recv.at[my_seq, core], back_rsem).start()

            @pl.when(jnp.logical_not(here))
            def _():
                remote(
                    back_send.at[at, other], back_recv.at[my_seq, core], back_ssem, back_rsem,
                    device(z_lo_, x_, core_, group, source_y),
                ).start()

        return unused

    lax.fori_loop(0, GROUPS, send_back, 0)
    await_bytes(back_recv, back_rsem)

    def put(at, unused):
        seq = group_ref[at]
        out_ref[at, pl.ds(0, HALF), :] = back_recv[seq, 0]
        out_ref[at, pl.ds(HALF, HALF), :] = back_recv[seq, 1]
        return unused

    lax.fori_loop(0, NB, put, 0)

    sent_all = query_y != y
    back_all = z_hi == 1

    @pl.when(sent_all)
    def _():
        await_bytes(q_send, q_ssem)
        await_bytes(rank_recv, m_ssem)

    @pl.when(jnp.logical_not(sent_all))
    def _():
        await_bytes(q_send.at[pl.ds(0, GROUPS - 1)], q_ssem)
        await_bytes(q_send.at[0, 0], q_ssem)
        await_bytes(rank_recv.at[0], m_ssem)
        await_bytes(rank_recv.at[1, pl.ds(0, GROUPS - 1)], m_ssem)

    @pl.when(back_all)
    def _():
        await_bytes(back_send, back_ssem)

    @pl.when(jnp.logical_not(back_all))
    def _():
        await_bytes(back_send.at[pl.ds(0, GROUPS - 1)], back_ssem)
        await_bytes(back_send.at[0, 0], back_ssem)

    @pl.when(stays)
    def _():
        await_bytes(krank_recv.at[pl.ds(0, GROUPS - 1)], km_ssem)
        for part in range(PARTS):
            await_bytes(kv_send.at[part, pl.ds(0, GROUPS - 1)], kv_ssem.at[part])

    @pl.when(jnp.logical_not(stays))
    def _():
        await_bytes(krank_recv, km_ssem)
        for part in range(PARTS):
            await_bytes(kv_send.at[part], kv_ssem.at[part])

    for part in range(PARTS):
        for which in range(4):
            ring_copy(part, which).wait_send()
            core_copy(part, which).wait_send()


def shards(query_rows, key_rows, value_rows, doc_lens, dest_group, block_pos):
    bf16, i32, f32 = jnp.bfloat16, jnp.int32, jnp.float32
    vmem = pl.BlockSpec(memory_space=pltpu.VMEM)
    smem = pl.BlockSpec(memory_space=pltpu.SMEM)
    dma = pltpu.SemaphoreType.DMA
    blocks = (NB, BLK, HEAD)
    out = pl.pallas_call(
        kernel,
        out_shape=jax.ShapeDtypeStruct(blocks, bf16),
        in_specs=[vmem, vmem, vmem, smem, smem, smem],
        out_specs=vmem,
        scratch_shapes=[
            pltpu.VMEM((GROUPS, 2, HALF, HEAD), bf16),
            pltpu.VMEM((2, GROUPS, HALF, HEAD), bf16),
            pltpu.VMEM((PARTS, GROUPS, 2, HALF, HEAD), bf16),
            pltpu.VMEM((GROUPS, 2, HALF, HEAD), bf16),
            pltpu.VMEM((GROUPS, 2, HALF, HEAD), bf16),
            pltpu.VMEM((PARTS, 2 * RING, 2, UNIT, HEAD), bf16),
            pltpu.VMEM((PARTS, 2 * RING, UNIT, HEAD), bf16),
            pltpu.VMEM((2, UNIT, HEAD), bf16),
            pltpu.VMEM((2, UNIT, HEAD), bf16),
            pltpu.VMEM((GROUPS, 1, HEAD), i32),
            pltpu.VMEM((2, GROUPS, 1, HEAD), i32),
            pltpu.VMEM((GROUPS, 1, HEAD), i32),
            pltpu.SMEM((2, GROUPS, 1, HEAD), i32),
            pltpu.SMEM((GROUPS, 1, HEAD), i32),
            pltpu.VMEM((2, 1, HEAD), i32),
            pltpu.VMEM((2, 1, HEAD), i32),
            pltpu.VMEM((2, UNIT, HEAD), f32),
            pltpu.VMEM((2, UNIT, 2 * HEAD), f32),
            pltpu.VMEM((2, NB, HALF, HEAD), bf16),
            pltpu.VMEM((GROUPS, 2, HALF, HEAD), bf16),
            pltpu.VMEM((GROUPS, 2, HALF, HEAD), bf16),
            dma, dma, dma, dma, dma, dma,
            dma((PARTS,)), dma((PARTS,)),
            dma((PARTS, 4)), dma((PARTS, 4)), dma((PARTS, 4)), dma((PARTS, 4)),
            dma, dma, dma, dma, dma((2,)),
        ],
        compiler_params=pltpu.CompilerParams(
            collective_id=0, has_side_effects=True, vmem_limit_bytes=48 * 2**20
        ),
        name="packed_attention",
    )(
        query_rows.reshape(blocks), key_rows.reshape(blocks), value_rows.reshape(blocks),
        doc_lens, dest_group, block_pos,
    )
    return out.reshape(NB * BLK, HEAD)


def solution(mesh):
    both = P(("dp", "ctx"))
    rows = P(("dp", "ctx"), None)
    return jax.shard_map(
        shards,
        mesh=mesh,
        in_specs=(rows, rows, rows, P("dp", None), both, both),
        out_specs=rows,
        check_vma=False,
    )
```

```python
import math

import jax
import jax.numpy as jnp
from jax import lax
from jax.experimental import pallas as pl
from jax.experimental.pallas import tpu as pltpu
from jax.sharding import PartitionSpec as P

HEAD = 128
BLK = 256
NB = 8
HALF = BLK // 2
RING = 4
GROUPS = 16
SELF = 6
SEG = NB * BLK
UNIT = NB * HALF
PARTS = 2
PIECE = BLK // PARTS
WIDTH = NB * PIECE
EXP_SCALE = math.log2(math.e) / math.sqrt(HEAD)
FAR = -(2.0**40)
EMPTY = -1e30
MESH = pl.DeviceIdType.MESH
NT = (((1,), (1,)), ((), ()))


def widened(left, right):
    return jnp.concatenate([left, right], axis=1)


def attend_tiles(tiles, query_of, key_of, value_of, mask_of, peak_ref, acc_ref):
    def scores_of(tile):
        rows, keys = tile
        found = lax.dot_general(
            query_of(rows), key_of(keys), NT, preferred_element_type=jnp.float32
        )
        return found if mask_of is None else jnp.where(mask_of(rows, keys), found, FAR)

    scores = scores_of(tiles[0])
    for at, (rows, keys) in enumerate(tiles):
        following = scores_of(tiles[at + 1]) if at + 1 < len(tiles) else None
        old_peak = peak_ref[rows, :]
        peak = jnp.maximum(old_peak, jnp.max(scores, axis=1, keepdims=True))
        factor = jnp.exp2((old_peak - peak) * EXP_SCALE)
        peaks = jnp.concatenate([peak] * (keys.size // HEAD), axis=1)
        weights = jnp.exp2((scores - peaks) * EXP_SCALE).astype(jnp.bfloat16)
        added = jnp.dot(weights, value_of(keys), preferred_element_type=jnp.float32)
        acc_ref[rows, :] = acc_ref[rows, :] * widened(factor, factor) + added
        peak_ref[rows, :] = peak
        scores = following


def kernel(
    q_hbm, k_hbm, v_hbm, len_ref, group_ref, pos_ref, out_ref,
    q_ref, k_ref, v_ref, q_send, q_low, q_high,
    kv_send, kv_recv_0, kv_recv_1, kv_all, key_doc, query_doc, queries,
    rank_send, rank_recv, rank_smem, doc_own, doc_recv,
    peak, acc, result_low, result_high, back_send_low, back_send_high, back_recv,
    in_sem, q_ssem, q_rsem, m_ssem, m_rsem, kv_ssem, kv_rsem,
    ring_ssem, ring_rsem, core_ssem, core_rsem, doc_ssem, doc_rsem,
    back_ssem, back_rsem, local_sem,
):
    dp = lax.axis_index("dp")
    ctx = lax.axis_index("ctx")
    z_lo, x, core = dp // 8, (dp // 2) % 4, dp % 2
    z_hi, y = ctx // RING, ctx % RING
    my_seq = z_lo * 8 + x * 2 + z_hi
    own_seg = core * RING + y
    stays = core == z_hi
    kv_recv = (kv_recv_0, kv_recv_1)
    q_recv = (q_low, q_high)
    result = (result_low, result_high)
    back_send = (back_send_low, back_send_high)

    def device(z_lo_, x_, core_, z_hi_, y_):
        return (z_lo_ * 8 + x_ * 2 + core_, z_hi_ * RING + y_)

    up = device(z_lo, x, core, z_hi, (y + 1) % RING)
    down = device(z_lo, x, core, z_hi, (y + 3) % RING)
    twin = device(z_lo, x, 1 - core, z_hi, y)

    def remote(src, dst, ssem, rsem, target):
        return pltpu.make_async_remote_copy(
            src_ref=src, dst_ref=dst, send_sem=ssem, recv_sem=rsem,
            device_id=target, device_id_type=MESH,
        )

    def await_bytes(ref, sem):
        pltpu.make_async_copy(ref, ref, sem).wait()

    loads = [
        pltpu.make_async_copy(src, dst, in_sem.at[at])
        for at, (src, dst) in enumerate(((q_hbm, q_ref), (k_hbm, k_ref), (v_hbm, v_ref)))
    ]
    for load in loads:
        load.start()

    barrier = pltpu.get_barrier_semaphore()
    for at in range(1, 32):
        peer = device(
            (z_lo + at % 2) % 2, (x + (at // 2) % 4) % 4, (core + (at // 8) % 2) % 2, (z_hi + at // 16) % 2, y
        )
        pl.semaphore_signal(barrier, inc=1, device_id=peer, device_id_type=MESH)
    for neighbour in (up, down):
        pl.semaphore_signal(barrier, inc=1, device_id=neighbour, device_id_type=MESH)

    lane = lax.broadcasted_iota(jnp.int32, (1, HEAD), 1)
    begin = jnp.zeros((1, HEAD), jnp.int32)
    until = jnp.full((1, HEAD), 1 << 20, jnp.int32)
    total = jnp.int32(0)
    for document in range(4):
        begin = jnp.where(lane == document, total, begin)
        total = total + len_ref[0, document]
        until = jnp.where(lane == document, total, until)
    doc_own[0] = begin
    doc_own[1] = until

    def arrival(seq):
        slot, rank = jnp.int32(0), jnp.int32(-1)
        for block in range(NB):
            hit = group_ref[block] == seq
            slot = jnp.where(hit, block, slot)
            rank = jnp.where(hit, pos_ref[block] % NB, rank)
        return slot, rank

    def offsets_of(at):
        z_step = (3 - at // 4 + at % 4) % 4
        return (2 + 3 * (at % 4)) % 4, z_step % 2, z_step // 2

    def target_of(at):
        x_step, z_step, other = offsets_of(at)
        return (z_lo + z_step) % 2, (x + x_step) % 4, (z_hi + other) % 2

    for load in loads:
        load.wait()

    def stage(at, unused):
        z_lo_, x_, seq_core = target_of(at)
        slot, rank = arrival(z_lo_ * 8 + x_ * 2 + seq_core)
        rank_send[at] = jnp.full((1, HEAD), rank, jnp.int32)
        block = q_ref[slot]
        q_send[at, 0] = block[:HALF]
        q_send[at, 1] = block[HALF:]
        keys, values = k_ref[slot], v_ref[slot]
        for part in range(PARTS):
            kv_send[part, at, 0] = keys[part * PIECE:(part + 1) * PIECE]
            kv_send[part, at, 1] = values[part * PIECE:(part + 1) * PIECE]
        return unused

    lax.fori_loop(0, GROUPS, stage, 0)
    pl.semaphore_wait(barrier, 33)

    remote(doc_own, doc_recv, doc_ssem, doc_rsem, twin).start()

    def to_or_here(here, src, dst, ssem, rsem, target):
        @pl.when(here)
        def _():
            pltpu.make_async_copy(src, dst, rsem).start()

        @pl.when(jnp.logical_not(here))
        def _():
            remote(src, dst, ssem, rsem, target).start()

    def send_ranks():
        def send(at, unused):
            z_lo_, x_, seq_core = target_of(at)
            for other in range(2):
                half = (core + other) % 2
                to_or_here(
                    at + other * GROUPS == SELF, rank_send.at[at], rank_recv.at[z_hi, dp], m_ssem, m_rsem,
                    device(z_lo_, x_, half, seq_core, y),
                )
            return unused

        lax.fori_loop(0, GROUPS, send, 0)

    def send_queries(plane):
        def send(at, unused):
            z_lo_, x_, seq_core = target_of(at)
            for other in range(2):
                rows = (core + other) % 2
                to_or_here(
                    at + other * GROUPS == SELF, q_send.at[at, rows], q_recv[plane].at[dp],
                    q_ssem, q_rsem.at[plane], device(z_lo_, x_, rows, seq_core, y),
                )
            return unused

        lax.fori_loop(0, GROUPS, send, 0)

    def queries_sent():
        await_bytes(q_send.at[pl.ds(0, GROUPS - 1)], q_ssem)
        await_bytes(q_send.at[0, 0], q_ssem)

    def send_keys(part):
        def send(at, unused):
            z_lo_, x_, seq_core = target_of(at)
            to_or_here(
                (at == SELF) & stays, kv_send.at[part, at], kv_recv[part].at[dp],
                kv_ssem.at[part], kv_rsem.at[part], device(z_lo_, x_, z_hi, seq_core, y),
            )
            return unused

        lax.fori_loop(0, GROUPS, send, 0)

    def keys_sent(part):
        @pl.when(stays)
        def _():
            await_bytes(kv_send.at[part, pl.ds(0, GROUPS - 1)], kv_ssem.at[part])

        @pl.when(jnp.logical_not(stays))
        def _():
            await_bytes(kv_send.at[part], kv_ssem.at[part])

    def issue(batch):
        @pl.when(z_hi == 0)
        def _():
            send_keys(batch) if batch < PARTS else send_queries(0)

        @pl.when(z_hi == 1)
        def _():
            send_queries(1) if batch == 0 else send_keys(batch - 1)

    def sent(batch):
        @pl.when(z_hi == 0)
        def _():
            keys_sent(batch) if batch < PARTS else queries_sent()

        @pl.when(z_hi == 1)
        def _():
            queries_sent() if batch == 0 else keys_sent(batch - 1)

    send_ranks()
    issue(0)

    remote(doc_own, doc_recv, doc_ssem, doc_rsem, twin).wait()
    begin = jnp.where(stays, doc_own[0], doc_recv[0])
    until = jnp.where(stays, doc_own[1], doc_recv[1])

    def places(first, size):
        return lax.broadcasted_iota(jnp.int32, (size, HEAD), 0) + first

    def key_mark(first, size):
        place = places(first, size)
        return jnp.where((place >= begin) & (place < until), 0.0, FAR).astype(jnp.bfloat16)

    def mark_keys(block, unused):
        rows = pl.ds(pl.multiple_of((block % NB) * PIECE, PIECE), PIECE)
        for part in range(PARTS):
            key_doc[part, block // NB, rows, :] = key_mark(block * BLK + part * PIECE, PIECE)
        return unused

    lax.fori_loop(0, 2 * RING * NB, mark_keys, 0)

    def query_seg(group):
        return y + group * RING

    def prepare(rank, unused):
        rows = pl.ds(pl.multiple_of(rank * HALF, HALF), HALF)
        lanes = lax.broadcasted_iota(jnp.int32, (HALF, HEAD), 1)
        for group in range(2):
            place = places(query_seg(group) * SEG + rank * BLK + core * HALF, HALF)
            inside = (place >= begin) & (place < until) & (lanes < 4)
            query_doc[group, rows, :] = jnp.where(inside, 1.0, 0.0).astype(jnp.bfloat16)
            peak[group, rows, :] = jnp.full((HALF, HEAD), EMPTY, jnp.float32)
            acc[group, rows, :] = jnp.zeros((HALF, 2 * HEAD), jnp.float32)
        return unused

    lax.fori_loop(0, NB, prepare, 0)

    await_bytes(rank_recv, m_rsem)
    ranks_in = pltpu.make_async_copy(rank_recv, rank_smem, local_sem)
    ranks_in.start()
    ranks_in.wait()

    def source_of(plane, rank):
        source = jnp.int32(0)
        for sender in range(GROUPS):
            source = jnp.where(rank_smem[plane, sender, 0, 0] == rank, sender, source)
        return source

    def take_queries(group):
        await_bytes(q_recv[group], q_rsem.at[group])

        def place(rank, unused):
            rows = pl.ds(pl.multiple_of(rank * HALF, HALF), HALF)
            queries[group, rows, :] = q_recv[group][source_of(group, rank)]
            return unused

        lax.fori_loop(0, NB, place, 0)

    def seg_at(kind, shift):
        return kind * RING + (y + shift) % RING

    def kv_at(part, seg):
        return kv_all.at[part, seg]

    def ring_copy(part, which):
        here = (
            kv_at(part, own_seg), kv_at(part, own_seg),
            kv_at(part, seg_at(core, 3)).at[0], kv_at(part, seg_at(core, 1)).at[1],
        )[which]
        return remote(here, here, ring_ssem.at[part, which], ring_rsem.at[part, which], (up, down)[which % 2])

    def ring_arrived(part, which):
        there = (
            kv_at(part, seg_at(core, 3)), kv_at(part, seg_at(core, 1)),
            kv_at(part, seg_at(core, 2)).at[0], kv_at(part, seg_at(core, 2)).at[1],
        )[which]
        await_bytes(there, ring_rsem.at[part, which])

    def shift_of(step):
        return (0, 3, 1, 2)[step]

    def core_copy(part, step):
        here = kv_at(part, seg_at(core, shift_of(step)))
        return remote(here, here, core_ssem.at[part, step], core_rsem.at[part, step], twin)

    def begin_part(part):
        await_bytes(kv_recv[part], kv_rsem.at[part])

        def place(rank, unused):
            rows = pl.ds(pl.multiple_of(rank * PIECE, PIECE), PIECE)
            source = source_of(core, rank)
            for which in range(2):
                kv_all[part, own_seg, which, rows, :] = kv_recv[part][source, which]
            return unused

        lax.fori_loop(0, NB, place, 0)
        ring_copy(part, 0).start()
        ring_copy(part, 1).start()
        core_copy(part, 0).start()

    def pass_on(part):
        ring_arrived(part, 0)
        ring_copy(part, 2).start()
        core_copy(part, 1).start()
        ring_arrived(part, 1)
        ring_copy(part, 3).start()
        core_copy(part, 2).start()

    def complete(part):
        ring_arrived(part, 2)
        ring_arrived(part, 3)
        core_copy(part, 3).start()

    def unit(part, seg, group, tiles, masked):
        def mask_of(rows, keys):
            row = lax.broadcasted_iota(jnp.int32, (rows.size, 1), 0) + rows.start
            key = lax.broadcasted_iota(jnp.int32, (1, keys.size), 1) + keys.start
            query_place = (row // HALF) * BLK + core * HALF + row % HALF
            return (key // PIECE) * BLK + part * PIECE + key % PIECE <= query_place

        attend_tiles(
            tiles,
            lambda rows: widened(queries[group, rows, :], query_doc[group, rows, :]),
            lambda keys: widened(kv_all[part, seg, 0, keys, :], key_doc[part, seg, keys, :]),
            lambda keys: widened(kv_all[part, seg, 1, keys, :], jnp.ones((keys.size, HEAD), jnp.bfloat16)),
            mask_of if masked else None,
            peak.at[group],
            acc.at[group],
        )

    def finish(group):
        def divide(rank, unused):
            both = acc[group, pl.ds(pl.multiple_of(rank * HALF, HALF), HALF), :]
            result[group][rank] = (both[:, :HEAD] / both[:, HEAD:]).astype(jnp.bfloat16)
            return unused

        lax.fori_loop(0, NB, divide, 0)

        def send(at, unused):
            x_step, z_step, other = offsets_of(at)
            z_lo_, x_, core_ = (z_lo + z_step) % 2, (x + x_step) % 4, (core + other) % 2
            rank = jnp.maximum(rank_smem[group, z_lo_ * 8 + x_ * 2 + core_, 0, 0], 0)
            back_send[group][at] = result[group][rank]
            to_or_here(
                (at == SELF) & (z_hi == group), back_send[group].at[at], back_recv.at[my_seq, core],
                back_ssem.at[group], back_rsem, device(z_lo_, x_, core_, group, y),
            )
            return unused

        lax.fori_loop(0, GROUPS, send, 0)

    def visits_of(part, kind, group, fresh, *steps):
        return [(part, kind, step, group, fresh) for step in steps]

    visits = (
        *visits_of(0, 0, 1, 1, 0, 1, 2, 3),
        *visits_of(1, 0, 1, 1, 0),
        *visits_of(0, 1, 1, 1, 0),
        *visits_of(1, 0, 1, 1, 1, 2),
        *visits_of(0, 1, 1, 1, 1, 2),
        *visits_of(0, 0, 0, 0, 0, 1, 2, 3),
        *visits_of(1, 0, 0, 0, 0, 1, 2),
        *visits_of(1, 0, 1, 1, 3),
        *visits_of(0, 1, 1, 1, 3),
        *visits_of(1, 0, 0, 0, 3),
        *visits_of(1, 1, 1, 1, 0, 1, 2, 3),
    )

    def go_on(batch):
        sent(batch - 1)
        issue(batch)

    def on(known, act, part):
        return (known, lambda: act(part))

    actions = {
        1: (on(0, pass_on, 0),),
        3: (on(0, complete, 0),),
        4: (on(None, go_on, 2), on(0, begin_part, 1), on(1, begin_part, 0)),
        6: (on(0, pass_on, 1), on(1, pass_on, 0)),
        8: (on(1, begin_part, 1),),
        10: (on(None, take_queries, 0),),
        12: (on(0, complete, 1), on(1, complete, 0)),
        16: (on(1, pass_on, 1),),
        19: (on(1, complete, 1),),
        20: (on(None, finish, 0),),
    }
    low, high, whole = pl.ds(0, UNIT // 2), pl.ds(UNIT // 2, UNIT // 2), pl.ds(0, WIDTH)
    half = pl.ds(0, WIDTH // 2)

    def pick(at, values):
        found = jnp.int32(values[0])
        for index in range(1, len(values)):
            found = jnp.where(at == index, values[index], found)
        return found

    def visit(at, unused):
        code = pick(at, [(((part * 2 + kind) * RING + step) * 2 + group) * 2 + fresh for part, kind, step, group, fresh in visits])
        part, kind, step, group, fresh = code // 32, (code // 16) % 2, (code // 4) % 4, (code // 2) % 2, code % 2
        for due, listed in actions.items():
            for core_known, act in listed:
                pl.when(at == due if core_known is None else (at == due) & (core == core_known))(act)

        seg = kind * RING + (y + pick(step, (0, 3, 1, 2))) % RING

        @pl.when((fresh == 1) & (kind != core))
        def _():
            await_bytes(kv_all.at[part, seg], core_rsem.at[part, step])

        wanted = query_seg(group)

        @pl.when(seg < wanted)
        def _():
            unit(part, seg, group, [(low, whole), (high, whole)], False)

        @pl.when(seg == wanted)
        def _():
            unit(part, seg, group, [(low, half), (high, whole)], True)

        return unused

    sent(0)
    issue(1)

    @pl.when(core == 0)
    def _():
        begin_part(0)

    take_queries(1)
    lax.fori_loop(0, len(visits), visit, 0)
    finish(1)

    await_bytes(back_recv, back_rsem)

    def put(at, unused):
        seq = group_ref[at]
        out_ref[at, pl.ds(0, HALF), :] = back_recv[seq, 0]
        out_ref[at, pl.ds(HALF, HALF), :] = back_recv[seq, 1]
        return unused

    lax.fori_loop(0, NB, put, 0)

    await_bytes(rank_recv.at[0], m_ssem)
    await_bytes(rank_recv.at[1, pl.ds(0, GROUPS - 1)], m_ssem)
    for group in range(2):
        @pl.when(z_hi == group)
        def _():
            await_bytes(back_send[group].at[pl.ds(0, GROUPS - 1)], back_ssem.at[group])

        @pl.when(z_hi != group)
        def _():
            await_bytes(back_send[group], back_ssem.at[group])

    sent(2)
    for part in range(PARTS):
        for which in range(4):
            ring_copy(part, which).wait_send()
            core_copy(part, which).wait_send()


def shards(query_rows, key_rows, value_rows, doc_lens, dest_group, block_pos):
    bf16, i32, f32 = jnp.bfloat16, jnp.int32, jnp.float32
    vmem = pl.BlockSpec(memory_space=pltpu.VMEM)
    smem = pl.BlockSpec(memory_space=pltpu.SMEM)
    anywhere = pl.BlockSpec(memory_space=pl.ANY)
    dma = pltpu.SemaphoreType.DMA
    blocks = (NB, BLK, HEAD)
    slots = (GROUPS, 2, PIECE, HEAD)
    out = pl.pallas_call(
        kernel,
        out_shape=jax.ShapeDtypeStruct(blocks, bf16),
        in_specs=[anywhere, anywhere, anywhere, smem, smem, smem],
        out_specs=vmem,
        scratch_shapes=[
            pltpu.VMEM(blocks, bf16),
            pltpu.VMEM(blocks, bf16),
            pltpu.VMEM(blocks, bf16),
            pltpu.VMEM((GROUPS, 2, HALF, HEAD), bf16),
            pltpu.VMEM((GROUPS, HALF, HEAD), bf16),
            pltpu.VMEM((GROUPS, HALF, HEAD), bf16),
            pltpu.VMEM((PARTS, *slots), bf16),
            *[pltpu.VMEM(slots, bf16) for _ in range(PARTS)],
            pltpu.VMEM((PARTS, 2 * RING, 2, WIDTH, HEAD), bf16),
            pltpu.VMEM((PARTS, 2 * RING, WIDTH, HEAD), bf16),
            pltpu.VMEM((2, UNIT, HEAD), bf16),
            pltpu.VMEM((2, UNIT, HEAD), bf16),
            pltpu.VMEM((GROUPS, 1, HEAD), i32),
            pltpu.VMEM((2, GROUPS, 1, HEAD), i32),
            pltpu.SMEM((2, GROUPS, 1, HEAD), i32),
            pltpu.VMEM((2, 1, HEAD), i32),
            pltpu.VMEM((2, 1, HEAD), i32),
            pltpu.VMEM((2, UNIT, HEAD), f32),
            pltpu.VMEM((2, UNIT, 2 * HEAD), f32),
            pltpu.VMEM((NB, HALF, HEAD), bf16),
            pltpu.VMEM((NB, HALF, HEAD), bf16),
            pltpu.VMEM((GROUPS, HALF, HEAD), bf16),
            pltpu.VMEM((GROUPS, HALF, HEAD), bf16),
            pltpu.VMEM((GROUPS, 2, HALF, HEAD), bf16),
            dma((3,)), dma, dma((2,)), dma, dma, dma((PARTS,)), dma((PARTS,)),
            dma((PARTS, 4)), dma((PARTS, 4)), dma((PARTS, 4)), dma((PARTS, 4)),
            dma, dma, dma((2,)), dma, dma,
        ],
        compiler_params=pltpu.CompilerParams(
            collective_id=0, has_side_effects=True, vmem_limit_bytes=52 * 2**20
        ),
        name="packed_attention",
    )(
        query_rows.reshape(blocks), key_rows.reshape(blocks), value_rows.reshape(blocks),
        doc_lens, dest_group, block_pos,
    )
    return out.reshape(NB * BLK, HEAD)


def solution(mesh):
    both = P(("dp", "ctx"))
    rows = P(("dp", "ctx"), None)
    return jax.shard_map(
        shards,
        mesh=mesh,
        in_specs=(rows, rows, rows, P("dp", None), both, both),
        out_specs=rows,
        check_vma=False,
    )
```

```python
import math

import jax
import jax.numpy as jnp
from jax import lax
from jax.experimental import pallas as pl
from jax.experimental.pallas import tpu as pltpu
from jax.sharding import PartitionSpec as P

HEAD = 128
BLK = 256
NB = 8
HALF = BLK // 2
RING = 4
GROUPS = 16
SELF = 6
SEG = NB * BLK
UNIT = NB * HALF
PARTS = 2
PIECE = BLK // PARTS
WIDTH = NB * PIECE
EXP_SCALE = math.log2(math.e) / math.sqrt(HEAD)
FAR = -(2.0**40)
EMPTY = -1e30
MESH = pl.DeviceIdType.MESH
NT = (((1,), (1,)), ((), ()))


def widened(left, right):
    return jnp.concatenate([left, right], axis=1)


def attend_tiles(tiles, query_of, key_of, value_of, mask_of, peak_ref, acc_ref):
    def scores_of(tile):
        rows, keys = tile
        found = lax.dot_general(
            query_of(rows), key_of(keys), NT, preferred_element_type=jnp.float32
        )
        return found if mask_of is None else jnp.where(mask_of(rows, keys), found, FAR)

    scores = scores_of(tiles[0])
    for at, (rows, keys) in enumerate(tiles):
        following = scores_of(tiles[at + 1]) if at + 1 < len(tiles) else None
        old_peak = peak_ref[rows, :]
        peak = jnp.maximum(old_peak, jnp.max(scores, axis=1, keepdims=True))
        factor = jnp.exp2((old_peak - peak) * EXP_SCALE)
        peaks = jnp.concatenate([peak] * (keys.size // HEAD), axis=1)
        weights = jnp.exp2((scores - peaks) * EXP_SCALE).astype(jnp.bfloat16)
        added = jnp.dot(weights, value_of(keys), preferred_element_type=jnp.float32)
        acc_ref[rows, :] = acc_ref[rows, :] * widened(factor, factor) + added
        peak_ref[rows, :] = peak
        scores = following


def kernel(
    q_hbm, k_hbm, v_hbm, len_ref, group_ref, pos_ref, out_ref,
    q_ref, k_ref, v_ref, q_send, q_low, q_high,
    kv_send, kv_recv_0, kv_recv_1, kv_all, key_doc, query_doc, queries,
    rank_send, rank_recv, rank_smem, doc_own, doc_recv,
    peak, acc, result_low, result_high, back_send_low, back_send_high, back_recv,
    in_sem, q_ssem, q_rsem, m_ssem, m_rsem, kv_ssem, kv_rsem,
    ring_ssem, ring_rsem, core_ssem, core_rsem, doc_ssem, doc_rsem,
    back_ssem, back_rsem, local_sem,
):
    dp = lax.axis_index("dp")
    ctx = lax.axis_index("ctx")
    z_lo, x, core = dp // 8, (dp // 2) % 4, dp % 2
    z_hi, y = ctx // RING, ctx % RING
    my_seq = z_lo * 8 + x * 2 + z_hi
    own_seg = core * RING + y
    stays = core == z_hi
    kv_recv = (kv_recv_0, kv_recv_1)
    q_recv = (q_low, q_high)
    result = (result_low, result_high)
    back_send = (back_send_low, back_send_high)

    def device(z_lo_, x_, core_, z_hi_, y_):
        return (z_lo_ * 8 + x_ * 2 + core_, z_hi_ * RING + y_)

    up = device(z_lo, x, core, z_hi, (y + 1) % RING)
    down = device(z_lo, x, core, z_hi, (y + 3) % RING)
    twin = device(z_lo, x, 1 - core, z_hi, y)

    def remote(src, dst, ssem, rsem, target):
        return pltpu.make_async_remote_copy(
            src_ref=src, dst_ref=dst, send_sem=ssem, recv_sem=rsem,
            device_id=target, device_id_type=MESH,
        )

    def await_bytes(ref, sem):
        pltpu.make_async_copy(ref, ref, sem).wait()

    loads = [
        pltpu.make_async_copy(src, dst, in_sem.at[at])
        for at, (src, dst) in enumerate(((q_hbm, q_ref), (k_hbm, k_ref), (v_hbm, v_ref)))
    ]
    for load in loads:
        load.start()

    barrier = pltpu.get_barrier_semaphore()
    for at in range(1, 32):
        peer = device(
            (z_lo + at % 2) % 2, (x + (at // 2) % 4) % 4, (core + (at // 8) % 2) % 2, (z_hi + at // 16) % 2, y
        )
        pl.semaphore_signal(barrier, inc=1, device_id=peer, device_id_type=MESH)
    for neighbour in (up, down):
        pl.semaphore_signal(barrier, inc=1, device_id=neighbour, device_id_type=MESH)

    lane = lax.broadcasted_iota(jnp.int32, (1, HEAD), 1)
    begin = jnp.zeros((1, HEAD), jnp.int32)
    until = jnp.full((1, HEAD), 1 << 20, jnp.int32)
    total = jnp.int32(0)
    for document in range(4):
        begin = jnp.where(lane == document, total, begin)
        total = total + len_ref[0, document]
        until = jnp.where(lane == document, total, until)
    doc_own[0] = begin
    doc_own[1] = until

    def arrival(seq):
        slot, rank = jnp.int32(0), jnp.int32(-1)
        for block in range(NB):
            hit = group_ref[block] == seq
            slot = jnp.where(hit, block, slot)
            rank = jnp.where(hit, pos_ref[block] % NB, rank)
        return slot, rank

    def offsets_of(at):
        z_step = (3 - at // 4 + at % 4) % 4
        return (2 + 3 * (at % 4)) % 4, z_step % 2, z_step // 2

    def target_of(at):
        x_step, z_step, other = offsets_of(at)
        return (z_lo + z_step) % 2, (x + x_step) % 4, (z_hi + other) % 2

    for load in loads:
        load.wait()

    def stage(at, unused):
        z_lo_, x_, seq_core = target_of(at)
        slot, rank = arrival(z_lo_ * 8 + x_ * 2 + seq_core)
        rank_send[at] = jnp.full((1, HEAD), rank, jnp.int32)
        block = q_ref[slot]
        q_send[at, 0] = block[:HALF]
        q_send[at, 1] = block[HALF:]
        keys, values = k_ref[slot], v_ref[slot]
        for part in range(PARTS):
            kv_send[part, at, 0] = keys[part * PIECE:(part + 1) * PIECE]
            kv_send[part, at, 1] = values[part * PIECE:(part + 1) * PIECE]
        return unused

    lax.fori_loop(0, GROUPS, stage, 0)
    pl.semaphore_wait(barrier, 33)

    remote(doc_own, doc_recv, doc_ssem, doc_rsem, twin).start()

    def to_or_here(here, src, dst, ssem, rsem, target):
        @pl.when(here)
        def _():
            pltpu.make_async_copy(src, dst, rsem).start()

        @pl.when(jnp.logical_not(here))
        def _():
            remote(src, dst, ssem, rsem, target).start()

    def send_ranks():
        def send(at, unused):
            z_lo_, x_, seq_core = target_of(at)
            for other in range(2):
                half = (core + other) % 2
                to_or_here(
                    at + other * GROUPS == SELF, rank_send.at[at], rank_recv.at[z_hi, dp], m_ssem, m_rsem,
                    device(z_lo_, x_, half, seq_core, y),
                )
            return unused

        lax.fori_loop(0, GROUPS, send, 0)

    def send_queries(plane):
        def send(at, unused):
            z_lo_, x_, seq_core = target_of(at)
            for other in range(2):
                rows = (core + other) % 2
                to_or_here(
                    at + other * GROUPS == SELF, q_send.at[at, rows], q_recv[plane].at[dp],
                    q_ssem, q_rsem.at[plane], device(z_lo_, x_, rows, seq_core, y),
                )
            return unused

        lax.fori_loop(0, GROUPS, send, 0)

    def queries_sent():
        await_bytes(q_send.at[pl.ds(0, GROUPS - 1)], q_ssem)
        await_bytes(q_send.at[0, 0], q_ssem)

    def send_keys(part):
        def send(at, unused):
            z_lo_, x_, seq_core = target_of(at)
            to_or_here(
                (at == SELF) & stays, kv_send.at[part, at], kv_recv[part].at[dp],
                kv_ssem.at[part], kv_rsem.at[part], device(z_lo_, x_, z_hi, seq_core, y),
            )
            return unused

        lax.fori_loop(0, GROUPS, send, 0)

    def keys_sent(part):
        @pl.when(stays)
        def _():
            await_bytes(kv_send.at[part, pl.ds(0, GROUPS - 1)], kv_ssem.at[part])

        @pl.when(jnp.logical_not(stays))
        def _():
            await_bytes(kv_send.at[part], kv_ssem.at[part])

    def issue(batch):
        @pl.when(z_hi == 0)
        def _():
            send_queries(0) if batch == 1 else send_keys(batch // 2)

        @pl.when(z_hi == 1)
        def _():
            send_queries(1) if batch == 0 else send_keys(batch - 1)

    def sent(batch):
        @pl.when(z_hi == 0)
        def _():
            queries_sent() if batch == 1 else keys_sent(batch // 2)

        @pl.when(z_hi == 1)
        def _():
            queries_sent() if batch == 0 else keys_sent(batch - 1)

    send_ranks()
    issue(0)

    remote(doc_own, doc_recv, doc_ssem, doc_rsem, twin).wait()
    begin = jnp.where(stays, doc_own[0], doc_recv[0])
    until = jnp.where(stays, doc_own[1], doc_recv[1])

    def places(first, size):
        return lax.broadcasted_iota(jnp.int32, (size, HEAD), 0) + first

    def key_mark(first, size):
        place = places(first, size)
        return jnp.where((place >= begin) & (place < until), 0.0, FAR).astype(jnp.bfloat16)

    def mark_keys(block, unused):
        rows = pl.ds(pl.multiple_of((block % NB) * PIECE, PIECE), PIECE)
        for part in range(PARTS):
            key_doc[part, block // NB, rows, :] = key_mark(block * BLK + part * PIECE, PIECE)
        return unused

    lax.fori_loop(0, 2 * RING * NB, mark_keys, 0)

    def query_seg(group):
        return y + group * RING

    def prepare(rank, unused):
        rows = pl.ds(pl.multiple_of(rank * HALF, HALF), HALF)
        lanes = lax.broadcasted_iota(jnp.int32, (HALF, HEAD), 1)
        for group in range(2):
            place = places(query_seg(group) * SEG + rank * BLK + core * HALF, HALF)
            inside = (place >= begin) & (place < until) & (lanes < 4)
            query_doc[group, rows, :] = jnp.where(inside, 1.0, 0.0).astype(jnp.bfloat16)
            peak[group, rows, :] = jnp.full((HALF, HEAD), EMPTY, jnp.float32)
            acc[group, rows, :] = jnp.zeros((HALF, 2 * HEAD), jnp.float32)
        return unused

    lax.fori_loop(0, NB, prepare, 0)

    await_bytes(rank_recv, m_rsem)
    ranks_in = pltpu.make_async_copy(rank_recv, rank_smem, local_sem)
    ranks_in.start()
    ranks_in.wait()

    def source_of(plane, rank):
        source = jnp.int32(0)
        for sender in range(GROUPS):
            source = jnp.where(rank_smem[plane, sender, 0, 0] == rank, sender, source)
        return source

    def take_queries(group):
        await_bytes(q_recv[group], q_rsem.at[group])

        def place(rank, unused):
            rows = pl.ds(pl.multiple_of(rank * HALF, HALF), HALF)
            queries[group, rows, :] = q_recv[group][source_of(group, rank)]
            return unused

        lax.fori_loop(0, NB, place, 0)

    def seg_at(kind, shift):
        return kind * RING + (y + shift) % RING

    def kv_at(part, seg):
        return kv_all.at[part, seg]

    def ring_copy(part, which):
        here = (
            kv_at(part, own_seg), kv_at(part, own_seg),
            kv_at(part, seg_at(core, 3)).at[0], kv_at(part, seg_at(core, 1)).at[1],
        )[which]
        return remote(here, here, ring_ssem.at[part, which], ring_rsem.at[part, which], (up, down)[which % 2])

    def ring_arrived(part, which):
        there = (
            kv_at(part, seg_at(core, 3)), kv_at(part, seg_at(core, 1)),
            kv_at(part, seg_at(core, 2)).at[0], kv_at(part, seg_at(core, 2)).at[1],
        )[which]
        await_bytes(there, ring_rsem.at[part, which])

    def shift_of(step):
        return (0, 3, 1, 2)[step]

    def core_copy(part, step):
        here = kv_at(part, seg_at(core, shift_of(step)))
        return remote(here, here, core_ssem.at[part, step], core_rsem.at[part, step], twin)

    def begin_part(part):
        await_bytes(kv_recv[part], kv_rsem.at[part])

        def place(rank, unused):
            rows = pl.ds(pl.multiple_of(rank * PIECE, PIECE), PIECE)
            source = source_of(core, rank)
            for which in range(2):
                kv_all[part, own_seg, which, rows, :] = kv_recv[part][source, which]
            return unused

        lax.fori_loop(0, NB, place, 0)
        ring_copy(part, 0).start()
        ring_copy(part, 1).start()
        core_copy(part, 0).start()

    def pass_on(part):
        ring_arrived(part, 0)
        ring_copy(part, 2).start()
        core_copy(part, 1).start()
        ring_arrived(part, 1)
        ring_copy(part, 3).start()
        core_copy(part, 2).start()

    def complete(part):
        ring_arrived(part, 2)
        ring_arrived(part, 3)
        core_copy(part, 3).start()

    def unit(part, seg, group, tiles, masked):
        def mask_of(rows, keys):
            row = lax.broadcasted_iota(jnp.int32, (rows.size, 1), 0) + rows.start
            key = lax.broadcasted_iota(jnp.int32, (1, keys.size), 1) + keys.start
            query_place = (row // HALF) * BLK + core * HALF + row % HALF
            return (key // PIECE) * BLK + part * PIECE + key % PIECE <= query_place

        attend_tiles(
            tiles,
            lambda rows: widened(queries[group, rows, :], query_doc[group, rows, :]),
            lambda keys: widened(kv_all[part, seg, 0, keys, :], key_doc[part, seg, keys, :]),
            lambda keys: widened(kv_all[part, seg, 1, keys, :], jnp.ones((keys.size, HEAD), jnp.bfloat16)),
            mask_of if masked else None,
            peak.at[group],
            acc.at[group],
        )

    def finish(group):
        def divide(rank, unused):
            both = acc[group, pl.ds(pl.multiple_of(rank * HALF, HALF), HALF), :]
            result[group][rank] = (both[:, :HEAD] / both[:, HEAD:]).astype(jnp.bfloat16)
            return unused

        lax.fori_loop(0, NB, divide, 0)

        def send(at, unused):
            x_step, z_step, other = offsets_of(at)
            z_lo_, x_, core_ = (z_lo + z_step) % 2, (x + x_step) % 4, (core + other) % 2
            rank = jnp.maximum(rank_smem[group, z_lo_ * 8 + x_ * 2 + core_, 0, 0], 0)
            back_send[group][at] = result[group][rank]
            to_or_here(
                (at == SELF) & (z_hi == group), back_send[group].at[at], back_recv.at[my_seq, core],
                back_ssem.at[group], back_rsem, device(z_lo_, x_, core_, group, y),
            )
            return unused

        lax.fori_loop(0, GROUPS, send, 0)

    def visits_of(part, kind, group, fresh, *steps):
        return [(part, kind, step, group, fresh) for step in steps]

    visits = (
        *visits_of(0, 0, 1, 1, 0, 1, 2, 3),
        *visits_of(0, 0, 0, 0, 0, 1, 2, 3),
        *visits_of(0, 1, 1, 1, 0, 1, 2, 3),
        *visits_of(1, 0, 1, 1, 0),
        *visits_of(1, 0, 0, 0, 0),
        *visits_of(1, 1, 1, 1, 0),
        *visits_of(1, 0, 1, 1, 1, 2),
        *visits_of(1, 0, 0, 0, 1, 2),
        *visits_of(1, 1, 1, 1, 1, 2),
        *visits_of(1, 0, 1, 1, 3),
        *visits_of(1, 0, 0, 0, 3),
        *visits_of(1, 1, 1, 1, 3),
    )

    def go_on(batch):
        sent(batch - 1)
        issue(batch)

    def on(known, act, part):
        return (known, lambda: act(part))

    actions = {
        1: (on(0, pass_on, 0),),
        2: (on(None, go_on, 2), on(1, begin_part, 0)),
        3: (on(0, complete, 0),),
        4: (on(None, take_queries, 0),),
        7: (on(1, pass_on, 0),),
        9: (on(None, begin_part, 1),),
        10: (on(1, complete, 0),),
        15: (on(None, pass_on, 1),),
        21: (on(None, complete, 1),),
        23: (on(None, finish, 0),),
    }
    low, high, whole = pl.ds(0, UNIT // 2), pl.ds(UNIT // 2, UNIT // 2), pl.ds(0, WIDTH)
    half = pl.ds(0, WIDTH // 2)

    def pick(at, values):
        found = jnp.int32(values[0])
        for index in range(1, len(values)):
            found = jnp.where(at == index, values[index], found)
        return found

    def visit(at, unused):
        code = pick(at, [(((part * 2 + kind) * RING + step) * 2 + group) * 2 + fresh for part, kind, step, group, fresh in visits])
        part, kind, step, group, fresh = code // 32, (code // 16) % 2, (code // 4) % 4, (code // 2) % 2, code % 2
        for due, listed in actions.items():
            for core_known, act in listed:
                pl.when(at == due if core_known is None else (at == due) & (core == core_known))(act)

        seg = kind * RING + (y + pick(step, (0, 3, 1, 2))) % RING

        @pl.when((fresh == 1) & (kind != core))
        def _():
            await_bytes(kv_all.at[part, seg], core_rsem.at[part, step])

        wanted = query_seg(group)

        @pl.when(seg < wanted)
        def _():
            unit(part, seg, group, [(low, whole), (high, whole)], False)

        @pl.when(seg == wanted)
        def _():
            unit(part, seg, group, [(low, half), (high, whole)], True)

        return unused

    sent(0)
    issue(1)

    @pl.when(core == 0)
    def _():
        begin_part(0)

    take_queries(1)
    lax.fori_loop(0, len(visits), visit, 0)
    finish(1)

    await_bytes(back_recv, back_rsem)

    def put(at, unused):
        seq = group_ref[at]
        out_ref[at, pl.ds(0, HALF), :] = back_recv[seq, 0]
        out_ref[at, pl.ds(HALF, HALF), :] = back_recv[seq, 1]
        return unused

    lax.fori_loop(0, NB, put, 0)

    await_bytes(rank_recv.at[0], m_ssem)
    await_bytes(rank_recv.at[1, pl.ds(0, GROUPS - 1)], m_ssem)
    for group in range(2):
        @pl.when(z_hi == group)
        def _():
            await_bytes(back_send[group].at[pl.ds(0, GROUPS - 1)], back_ssem.at[group])

        @pl.when(z_hi != group)
        def _():
            await_bytes(back_send[group], back_ssem.at[group])

    sent(2)
    for part in range(PARTS):
        for which in range(4):
            ring_copy(part, which).wait_send()
            core_copy(part, which).wait_send()


def shards(query_rows, key_rows, value_rows, doc_lens, dest_group, block_pos):
    bf16, i32, f32 = jnp.bfloat16, jnp.int32, jnp.float32
    vmem = pl.BlockSpec(memory_space=pltpu.VMEM)
    smem = pl.BlockSpec(memory_space=pltpu.SMEM)
    anywhere = pl.BlockSpec(memory_space=pl.ANY)
    dma = pltpu.SemaphoreType.DMA
    blocks = (NB, BLK, HEAD)
    slots = (GROUPS, 2, PIECE, HEAD)
    out = pl.pallas_call(
        kernel,
        out_shape=jax.ShapeDtypeStruct(blocks, bf16),
        in_specs=[anywhere, anywhere, anywhere, smem, smem, smem],
        out_specs=vmem,
        scratch_shapes=[
            pltpu.VMEM(blocks, bf16),
            pltpu.VMEM(blocks, bf16),
            pltpu.VMEM(blocks, bf16),
            pltpu.VMEM((GROUPS, 2, HALF, HEAD), bf16),
            pltpu.VMEM((GROUPS, HALF, HEAD), bf16),
            pltpu.VMEM((GROUPS, HALF, HEAD), bf16),
            pltpu.VMEM((PARTS, *slots), bf16),
            *[pltpu.VMEM(slots, bf16) for _ in range(PARTS)],
            pltpu.VMEM((PARTS, 2 * RING, 2, WIDTH, HEAD), bf16),
            pltpu.VMEM((PARTS, 2 * RING, WIDTH, HEAD), bf16),
            pltpu.VMEM((2, UNIT, HEAD), bf16),
            pltpu.VMEM((2, UNIT, HEAD), bf16),
            pltpu.VMEM((GROUPS, 1, HEAD), i32),
            pltpu.VMEM((2, GROUPS, 1, HEAD), i32),
            pltpu.SMEM((2, GROUPS, 1, HEAD), i32),
            pltpu.VMEM((2, 1, HEAD), i32),
            pltpu.VMEM((2, 1, HEAD), i32),
            pltpu.VMEM((2, UNIT, HEAD), f32),
            pltpu.VMEM((2, UNIT, 2 * HEAD), f32),
            pltpu.VMEM((NB, HALF, HEAD), bf16),
            pltpu.VMEM((NB, HALF, HEAD), bf16),
            pltpu.VMEM((GROUPS, HALF, HEAD), bf16),
            pltpu.VMEM((GROUPS, HALF, HEAD), bf16),
            pltpu.VMEM((GROUPS, 2, HALF, HEAD), bf16),
            dma((3,)), dma, dma((2,)), dma, dma, dma((PARTS,)), dma((PARTS,)),
            dma((PARTS, 4)), dma((PARTS, 4)), dma((PARTS, 4)), dma((PARTS, 4)),
            dma, dma, dma((2,)), dma, dma,
        ],
        compiler_params=pltpu.CompilerParams(
            collective_id=0, has_side_effects=True, vmem_limit_bytes=52 * 2**20
        ),
        name="packed_attention",
    )(
        query_rows.reshape(blocks), key_rows.reshape(blocks), value_rows.reshape(blocks),
        doc_lens, dest_group, block_pos,
    )
    return out.reshape(NB * BLK, HEAD)


def solution(mesh):
    both = P(("dp", "ctx"))
    rows = P(("dp", "ctx"), None)
    return jax.shard_map(
        shards,
        mesh=mesh,
        in_specs=(rows, rows, rows, P("dp", None), both, both),
        out_specs=rows,
        check_vma=False,
    )
```

```python
import math

import jax
import jax.numpy as jnp
from jax import lax
from jax.experimental import pallas as pl
from jax.experimental.pallas import tpu as pltpu
from jax.sharding import PartitionSpec as P

HEAD = 128
BLK = 256
NB = 8
HALF = BLK // 2
RING = 4
GROUPS = 16
SELF = 6
SEG = NB * BLK
UNIT = NB * HALF
PARTS = 2
PIECE = BLK // PARTS
WIDTH = NB * PIECE
EXP_SCALE = math.log2(math.e) / math.sqrt(HEAD)
FAR = -(2.0**40)
EMPTY = -1e30
MESH = pl.DeviceIdType.MESH
NT = (((1,), (1,)), ((), ()))


def widened(left, right):
    return jnp.concatenate([left, right], axis=1)


def attend_tiles(tiles, query_of, key_of, value_of, mask_of, peak_ref, acc_ref):
    def scores_of(tile):
        rows, keys = tile
        found = lax.dot_general(
            query_of(rows), key_of(keys), NT, preferred_element_type=jnp.float32
        )
        return found if mask_of is None else jnp.where(mask_of(rows, keys), found, FAR)

    scores = scores_of(tiles[0])
    for at, (rows, keys) in enumerate(tiles):
        following = scores_of(tiles[at + 1]) if at + 1 < len(tiles) else None
        old_peak = peak_ref[rows, :]
        peak = jnp.maximum(old_peak, jnp.max(scores, axis=1, keepdims=True))
        factor = jnp.exp2((old_peak - peak) * EXP_SCALE)
        peaks = jnp.concatenate([peak] * (keys.size // HEAD), axis=1)
        weights = jnp.exp2((scores - peaks) * EXP_SCALE).astype(jnp.bfloat16)
        added = jnp.dot(weights, value_of(keys), preferred_element_type=jnp.float32)
        acc_ref[rows, :] = acc_ref[rows, :] * widened(factor, factor) + added
        peak_ref[rows, :] = peak
        scores = following


def kernel(
    q_hbm, k_hbm, v_hbm, len_ref, group_ref, pos_ref, out_ref,
    q_ref, k_ref, v_ref, q_send, q_low, q_high,
    kv_send, kv_recv_0, kv_recv_1, kv_all, key_doc, query_doc, queries,
    rank_send, rank_recv, rank_smem, doc_own, doc_recv,
    peak, acc, result_low, result_high, back_send_low, back_send_high, back_recv,
    in_sem, q_ssem, q_rsem, m_ssem, m_rsem, kv_ssem, kv_rsem,
    ring_ssem, ring_rsem, core_ssem, core_rsem, doc_ssem, doc_rsem,
    back_ssem, back_rsem, local_sem, t_ssem, t_rsem,
):
    dp = lax.axis_index("dp")
    ctx = lax.axis_index("ctx")
    z_lo, x, core = dp // 8, (dp // 2) % 4, dp % 2
    z_hi, y = ctx // RING, ctx % RING
    my_seq = z_lo * 8 + x * 2 + z_hi
    own_seg = core * RING + y
    stays = core == z_hi
    kv_recv = (kv_recv_0, kv_recv_1)
    q_recv = (q_low, q_high)
    result = (result_low, result_high)
    back_send = (back_send_low, back_send_high)

    def device(z_lo_, x_, core_, z_hi_, y_):
        return (z_lo_ * 8 + x_ * 2 + core_, z_hi_ * RING + y_)

    up = device(z_lo, x, core, z_hi, (y + 1) % RING)
    down = device(z_lo, x, core, z_hi, (y + 3) % RING)
    twin = device(z_lo, x, 1 - core, z_hi, y)

    def remote(src, dst, ssem, rsem, target):
        return pltpu.make_async_remote_copy(
            src_ref=src, dst_ref=dst, send_sem=ssem, recv_sem=rsem,
            device_id=target, device_id_type=MESH,
        )

    def await_bytes(ref, sem):
        pltpu.make_async_copy(ref, ref, sem).wait()

    loads = [
        pltpu.make_async_copy(src, dst, in_sem.at[at])
        for at, (src, dst) in enumerate(((q_hbm, q_ref), (k_hbm, k_ref), (v_hbm, v_ref)))
    ]
    for load in loads:
        load.start()

    barrier = pltpu.get_barrier_semaphore()
    for at in range(1, 32):
        peer = device(
            (z_lo + at % 2) % 2, (x + (at // 2) % 4) % 4, (core + (at // 8) % 2) % 2, (z_hi + at // 16) % 2, y
        )
        pl.semaphore_signal(barrier, inc=1, device_id=peer, device_id_type=MESH)
    for neighbour in (up, down):
        pl.semaphore_signal(barrier, inc=1, device_id=neighbour, device_id_type=MESH)

    lane = lax.broadcasted_iota(jnp.int32, (1, HEAD), 1)
    begin = jnp.zeros((1, HEAD), jnp.int32)
    until = jnp.full((1, HEAD), 1 << 20, jnp.int32)
    total = jnp.int32(0)
    for document in range(4):
        begin = jnp.where(lane == document, total, begin)
        total = total + len_ref[0, document]
        until = jnp.where(lane == document, total, until)
    doc_own[0] = begin
    doc_own[1] = until

    def arrival(seq):
        slot, rank = jnp.int32(0), jnp.int32(-1)
        for block in range(NB):
            hit = group_ref[block] == seq
            slot = jnp.where(hit, block, slot)
            rank = jnp.where(hit, pos_ref[block] % NB, rank)
        return slot, rank

    def offsets_of(at):
        z_step = (3 - at // 4 + at % 4) % 4
        return (2 + 3 * (at % 4)) % 4, z_step % 2, z_step // 2

    def target_of(at):
        x_step, z_step, other = offsets_of(at)
        return (z_lo + z_step) % 2, (x + x_step) % 4, (z_hi + other) % 2

    for load in loads:
        load.wait()

    def stage(at, unused):
        z_lo_, x_, seq_core = target_of(at)
        slot, rank = arrival(z_lo_ * 8 + x_ * 2 + seq_core)
        rank_send[at] = jnp.full((1, HEAD), rank, jnp.int32)
        block = q_ref[slot]
        q_send[at, 0] = block[:HALF]
        q_send[at, 1] = block[HALF:]
        keys, values = k_ref[slot], v_ref[slot]
        for part in range(PARTS):
            kv_send[part, at, 0] = keys[part * PIECE:(part + 1) * PIECE]
            kv_send[part, at, 1] = values[part * PIECE:(part + 1) * PIECE]
        return unused

    lax.fori_loop(0, GROUPS, stage, 0)
    pl.semaphore_wait(barrier, 33)

    remote(doc_own, doc_recv, doc_ssem, doc_rsem, twin).start()

    def to_or_here(here, src, dst, ssem, rsem, target):
        @pl.when(here)
        def _():
            pltpu.make_async_copy(src, dst, rsem).start()

        @pl.when(jnp.logical_not(here))
        def _():
            remote(src, dst, ssem, rsem, target).start()

    def send_ranks():
        def send(at, unused):
            z_lo_, x_, seq_core = target_of(at)
            to_or_here(
                (at == SELF) & stays, rank_send.at[at], rank_recv.at[z_hi, dp], m_ssem, m_rsem,
                device(z_lo_, x_, z_hi, seq_core, y),
            )
            return unused

        lax.fori_loop(0, GROUPS, send, 0)

    def send_queries(plane):
        def send(at, unused):
            z_lo_, x_, seq_core = target_of(at)
            for other in range(2):
                rows = (core + other) % 2
                to_or_here(
                    at + other * GROUPS == SELF, q_send.at[at, rows], q_recv[plane].at[dp],
                    q_ssem, q_rsem.at[plane], device(z_lo_, x_, rows, seq_core, y),
                )
            return unused

        lax.fori_loop(0, GROUPS, send, 0)

    def queries_sent():
        await_bytes(q_send.at[pl.ds(0, GROUPS - 1)], q_ssem)
        await_bytes(q_send.at[0, 0], q_ssem)

    def send_keys(part):
        def send(at, unused):
            z_lo_, x_, seq_core = target_of(at)
            to_or_here(
                (at == SELF) & stays, kv_send.at[part, at], kv_recv[part].at[dp],
                kv_ssem.at[part], kv_rsem.at[part], device(z_lo_, x_, z_hi, seq_core, y),
            )
            return unused

        lax.fori_loop(0, GROUPS, send, 0)

    def keys_sent(part):
        @pl.when(stays)
        def _():
            await_bytes(kv_send.at[part, pl.ds(0, GROUPS - 1)], kv_ssem.at[part])

        @pl.when(jnp.logical_not(stays))
        def _():
            await_bytes(kv_send.at[part], kv_ssem.at[part])

    def issue(batch):
        @pl.when(z_hi == 0)
        def _():
            send_queries(0) if batch == 1 else send_keys(batch // 2)

        @pl.when(z_hi == 1)
        def _():
            send_queries(1) if batch == 0 else send_keys(batch - 1)

    def sent(batch):
        @pl.when(z_hi == 0)
        def _():
            queries_sent() if batch == 1 else keys_sent(batch // 2)

        @pl.when(z_hi == 1)
        def _():
            queries_sent() if batch == 0 else keys_sent(batch - 1)

    send_ranks()
    issue(0)

    remote(doc_own, doc_recv, doc_ssem, doc_rsem, twin).wait()
    begin = jnp.where(stays, doc_own[0], doc_recv[0])
    until = jnp.where(stays, doc_own[1], doc_recv[1])

    def places(first, size):
        return lax.broadcasted_iota(jnp.int32, (size, HEAD), 0) + first

    def key_mark(first, size):
        place = places(first, size)
        return jnp.where((place >= begin) & (place < until), 0.0, FAR).astype(jnp.bfloat16)

    def mark_keys(block, unused):
        rows = pl.ds(pl.multiple_of((block % NB) * PIECE, PIECE), PIECE)
        for part in range(PARTS):
            key_doc[part, block // NB, rows, :] = key_mark(block * BLK + part * PIECE, PIECE)
        return unused

    lax.fori_loop(0, 2 * RING * NB, mark_keys, 0)

    def query_seg(group):
        return y + group * RING

    def prepare(rank, unused):
        rows = pl.ds(pl.multiple_of(rank * HALF, HALF), HALF)
        lanes = lax.broadcasted_iota(jnp.int32, (HALF, HEAD), 1)
        for group in range(2):
            place = places(query_seg(group) * SEG + rank * BLK + core * HALF, HALF)
            inside = (place >= begin) & (place < until) & (lanes < 4)
            query_doc[group, rows, :] = jnp.where(inside, 1.0, 0.0).astype(jnp.bfloat16)
            peak[group, rows, :] = jnp.full((HALF, HEAD), EMPTY, jnp.float32)
            acc[group, rows, :] = jnp.zeros((HALF, 2 * HEAD), jnp.float32)
        return unused

    lax.fori_loop(0, NB, prepare, 0)

    await_bytes(rank_recv.at[core], m_rsem)
    shared = remote(rank_recv.at[core], rank_recv.at[core], t_ssem, t_rsem, twin)
    shared.start()
    shared.wait_send()
    await_bytes(rank_recv.at[1 - core], t_rsem)
    ranks_in = pltpu.make_async_copy(rank_recv, rank_smem, local_sem)
    ranks_in.start()
    ranks_in.wait()

    def source_of(plane, rank):
        source = jnp.int32(0)
        for sender in range(GROUPS):
            source = jnp.where(rank_smem[plane, sender, 0, 0] == rank, sender, source)
        return source

    def take_queries(group):
        await_bytes(q_recv[group], q_rsem.at[group])

        def place(rank, unused):
            rows = pl.ds(pl.multiple_of(rank * HALF, HALF), HALF)
            queries[group, rows, :] = q_recv[group][source_of(group, rank)]
            return unused

        lax.fori_loop(0, NB, place, 0)

    def seg_at(kind, shift):
        return kind * RING + (y + shift) % RING

    def kv_at(part, seg):
        return kv_all.at[part, seg]

    def ring_copy(part, which):
        here = (
            kv_at(part, own_seg), kv_at(part, own_seg),
            kv_at(part, seg_at(core, 3)).at[0], kv_at(part, seg_at(core, 1)).at[1],
        )[which]
        return remote(here, here, ring_ssem.at[part, which], ring_rsem.at[part, which], (up, down)[which % 2])

    def ring_arrived(part, which):
        there = (
            kv_at(part, seg_at(core, 3)), kv_at(part, seg_at(core, 1)),
            kv_at(part, seg_at(core, 2)).at[0], kv_at(part, seg_at(core, 2)).at[1],
        )[which]
        await_bytes(there, ring_rsem.at[part, which])

    def shift_of(step):
        return (0, 3, 1, 2)[step]

    def core_copy(part, step):
        here = kv_at(part, seg_at(core, shift_of(step)))
        return remote(here, here, core_ssem.at[part, step], core_rsem.at[part, step], twin)

    def begin_part(part):
        await_bytes(kv_recv[part], kv_rsem.at[part])

        def place(rank, unused):
            rows = pl.ds(pl.multiple_of(rank * PIECE, PIECE), PIECE)
            source = source_of(core, rank)
            for which in range(2):
                kv_all[part, own_seg, which, rows, :] = kv_recv[part][source, which]
            return unused

        lax.fori_loop(0, NB, place, 0)
        ring_copy(part, 0).start()
        ring_copy(part, 1).start()
        core_copy(part, 0).start()

    def pass_on(part):
        ring_arrived(part, 0)
        ring_copy(part, 2).start()
        core_copy(part, 1).start()
        ring_arrived(part, 1)
        ring_copy(part, 3).start()
        core_copy(part, 2).start()

    def complete(part):
        ring_arrived(part, 2)
        ring_arrived(part, 3)
        core_copy(part, 3).start()

    def unit(part, seg, group, tiles, masked):
        def mask_of(rows, keys):
            row = lax.broadcasted_iota(jnp.int32, (rows.size, 1), 0) + rows.start
            key = lax.broadcasted_iota(jnp.int32, (1, keys.size), 1) + keys.start
            query_place = (row // HALF) * BLK + core * HALF + row % HALF
            return (key // PIECE) * BLK + part * PIECE + key % PIECE <= query_place

        attend_tiles(
            tiles,
            lambda rows: widened(queries[group, rows, :], query_doc[group, rows, :]),
            lambda keys: widened(kv_all[part, seg, 0, keys, :], key_doc[part, seg, keys, :]),
            lambda keys: widened(kv_all[part, seg, 1, keys, :], jnp.ones((keys.size, HEAD), jnp.bfloat16)),
            mask_of if masked else None,
            peak.at[group],
            acc.at[group],
        )

    def finish(group):
        def divide(rank, unused):
            both = acc[group, pl.ds(pl.multiple_of(rank * HALF, HALF), HALF), :]
            result[group][rank] = (both[:, :HEAD] / both[:, HEAD:]).astype(jnp.bfloat16)
            return unused

        lax.fori_loop(0, NB, divide, 0)

        def send(at, unused):
            x_step, z_step, other = offsets_of(at)
            z_lo_, x_, core_ = (z_lo + z_step) % 2, (x + x_step) % 4, (core + other) % 2
            rank = jnp.maximum(rank_smem[group, z_lo_ * 8 + x_ * 2 + core_, 0, 0], 0)
            back_send[group][at] = result[group][rank]
            to_or_here(
                (at == SELF) & (z_hi == group), back_send[group].at[at], back_recv.at[my_seq, core],
                back_ssem.at[group], back_rsem, device(z_lo_, x_, core_, group, y),
            )
            return unused

        lax.fori_loop(0, GROUPS, send, 0)

    def visits_of(part, kind, group, fresh, *steps):
        return [(part, kind, step, group, fresh) for step in steps]

    visits = (
        *visits_of(0, 0, 1, 1, 0, 1, 2, 3),
        *visits_of(0, 0, 0, 0, 0, 1, 2, 3),
        *visits_of(0, 1, 1, 1, 0, 1, 2, 3),
        *visits_of(1, 0, 1, 1, 0),
        *visits_of(1, 0, 0, 0, 0),
        *visits_of(1, 1, 1, 1, 0),
        *visits_of(1, 0, 1, 1, 1, 2),
        *visits_of(1, 0, 0, 0, 1, 2),
        *visits_of(1, 1, 1, 1, 1, 2),
        *visits_of(1, 0, 1, 1, 3),
        *visits_of(1, 0, 0, 0, 3),
        *visits_of(1, 1, 1, 1, 3),
    )

    def go_on(batch):
        sent(batch - 1)
        issue(batch)

    def on(known, act, part):
        return (known, lambda: act(part))

    actions = {
        1: (on(0, pass_on, 0),),
        2: (on(None, go_on, 2), on(1, begin_part, 0)),
        3: (on(0, complete, 0),),
        4: (on(None, take_queries, 0),),
        7: (on(1, pass_on, 0),),
        10: (on(1, complete, 0), on(None, begin_part, 1)),
        15: (on(None, pass_on, 1),),
        21: (on(None, complete, 1),),
        23: (on(None, finish, 0),),
    }
    low, high, whole = pl.ds(0, UNIT // 2), pl.ds(UNIT // 2, UNIT // 2), pl.ds(0, WIDTH)
    half = pl.ds(0, WIDTH // 2)

    def pick(at, values):
        found = jnp.int32(values[0])
        for index in range(1, len(values)):
            found = jnp.where(at == index, values[index], found)
        return found

    def visit(at, unused):
        code = pick(at, [(((part * 2 + kind) * RING + step) * 2 + group) * 2 + fresh for part, kind, step, group, fresh in visits])
        part, kind, step, group, fresh = code // 32, (code // 16) % 2, (code // 4) % 4, (code // 2) % 2, code % 2
        for due, listed in actions.items():
            for core_known, act in listed:
                pl.when(at == due if core_known is None else (at == due) & (core == core_known))(act)

        seg = kind * RING + (y + pick(step, (0, 3, 1, 2))) % RING

        @pl.when((fresh == 1) & (kind != core))
        def _():
            await_bytes(kv_all.at[part, seg], core_rsem.at[part, step])

        wanted = query_seg(group)

        @pl.when(seg < wanted)
        def _():
            unit(part, seg, group, [(low, whole), (high, whole)], False)

        @pl.when(seg == wanted)
        def _():
            unit(part, seg, group, [(low, half), (high, whole)], True)

        return unused

    sent(0)
    issue(1)

    @pl.when(core == 0)
    def _():
        begin_part(0)

    take_queries(1)
    lax.fori_loop(0, len(visits), visit, 0)
    finish(1)

    await_bytes(back_recv, back_rsem)

    def put(at, unused):
        seq = group_ref[at]
        out_ref[at, pl.ds(0, HALF), :] = back_recv[seq, 0]
        out_ref[at, pl.ds(HALF, HALF), :] = back_recv[seq, 1]
        return unused

    lax.fori_loop(0, NB, put, 0)

    @pl.when(stays)
    def _():
        await_bytes(rank_recv.at[0, pl.ds(0, GROUPS - 1)], m_ssem)

    @pl.when(jnp.logical_not(stays))
    def _():
        await_bytes(rank_recv.at[0], m_ssem)

    for group in range(2):
        @pl.when(z_hi == group)
        def _():
            await_bytes(back_send[group].at[pl.ds(0, GROUPS - 1)], back_ssem.at[group])

        @pl.when(z_hi != group)
        def _():
            await_bytes(back_send[group], back_ssem.at[group])

    sent(2)
    for part in range(PARTS):
        for which in range(4):
            ring_copy(part, which).wait_send()
            core_copy(part, which).wait_send()


def shards(query_rows, key_rows, value_rows, doc_lens, dest_group, block_pos):
    bf16, i32, f32 = jnp.bfloat16, jnp.int32, jnp.float32
    vmem = pl.BlockSpec(memory_space=pltpu.VMEM)
    smem = pl.BlockSpec(memory_space=pltpu.SMEM)
    anywhere = pl.BlockSpec(memory_space=pl.ANY)
    dma = pltpu.SemaphoreType.DMA
    blocks = (NB, BLK, HEAD)
    slots = (GROUPS, 2, PIECE, HEAD)
    out = pl.pallas_call(
        kernel,
        out_shape=jax.ShapeDtypeStruct(blocks, bf16),
        in_specs=[anywhere, anywhere, anywhere, smem, smem, smem],
        out_specs=vmem,
        scratch_shapes=[
            pltpu.VMEM(blocks, bf16),
            pltpu.VMEM(blocks, bf16),
            pltpu.VMEM(blocks, bf16),
            pltpu.VMEM((GROUPS, 2, HALF, HEAD), bf16),
            pltpu.VMEM((GROUPS, HALF, HEAD), bf16),
            pltpu.VMEM((GROUPS, HALF, HEAD), bf16),
            pltpu.VMEM((PARTS, *slots), bf16),
            *[pltpu.VMEM(slots, bf16) for _ in range(PARTS)],
            pltpu.VMEM((PARTS, 2 * RING, 2, WIDTH, HEAD), bf16),
            pltpu.VMEM((PARTS, 2 * RING, WIDTH, HEAD), bf16),
            pltpu.VMEM((2, UNIT, HEAD), bf16),
            pltpu.VMEM((2, UNIT, HEAD), bf16),
            pltpu.VMEM((GROUPS, 1, HEAD), i32),
            pltpu.VMEM((2, GROUPS, 1, HEAD), i32),
            pltpu.SMEM((2, GROUPS, 1, HEAD), i32),
            pltpu.VMEM((2, 1, HEAD), i32),
            pltpu.VMEM((2, 1, HEAD), i32),
            pltpu.VMEM((2, UNIT, HEAD), f32),
            pltpu.VMEM((2, UNIT, 2 * HEAD), f32),
            pltpu.VMEM((NB, HALF, HEAD), bf16),
            pltpu.VMEM((NB, HALF, HEAD), bf16),
            pltpu.VMEM((GROUPS, HALF, HEAD), bf16),
            pltpu.VMEM((GROUPS, HALF, HEAD), bf16),
            pltpu.VMEM((GROUPS, 2, HALF, HEAD), bf16),
            dma((3,)), dma, dma((2,)), dma, dma, dma((PARTS,)), dma((PARTS,)),
            dma((PARTS, 4)), dma((PARTS, 4)), dma((PARTS, 4)), dma((PARTS, 4)),
            dma, dma, dma((2,)), dma, dma, dma, dma,
        ],
        compiler_params=pltpu.CompilerParams(
            collective_id=0, has_side_effects=True, vmem_limit_bytes=52 * 2**20
        ),
        name="packed_attention",
    )(
        query_rows.reshape(blocks), key_rows.reshape(blocks), value_rows.reshape(blocks),
        doc_lens, dest_group, block_pos,
    )
    return out.reshape(NB * BLK, HEAD)


def solution(mesh):
    both = P(("dp", "ctx"))
    rows = P(("dp", "ctx"), None)
    return jax.shard_map(
        shards,
        mesh=mesh,
        in_specs=(rows, rows, rows, P("dp", None), both, both),
        out_specs=rows,
        check_vma=False,
    )
```

```python
import math

import jax
import jax.numpy as jnp
from jax import lax
from jax.experimental import pallas as pl
from jax.experimental.pallas import tpu as pltpu
from jax.sharding import PartitionSpec as P

HEAD = 128
BLK = 256
NB = 8
HALF = BLK // 2
RING = 4
GROUPS = 16
SELF = 6
SEG = NB * BLK
UNIT = NB * HALF
PARTS = 2
PIECE = BLK // PARTS
WIDTH = NB * PIECE
EXP_SCALE = math.log2(math.e) / math.sqrt(HEAD)
FAR = -(2.0**40)
EMPTY = -1e30
MESH = pl.DeviceIdType.MESH
NT = (((1,), (1,)), ((), ()))


def widened(left, right):
    return jnp.concatenate([left, right], axis=1)


def attend_tiles(tiles, query_of, key_of, value_of, mask_of, peak_ref, acc_ref):
    def scores_of(tile):
        rows, keys = tile
        found = lax.dot_general(
            query_of(rows), key_of(keys), NT, preferred_element_type=jnp.float32
        )
        return found if mask_of is None else jnp.where(mask_of(rows, keys), found, FAR)

    scores = scores_of(tiles[0])
    for at, (rows, keys) in enumerate(tiles):
        following = scores_of(tiles[at + 1]) if at + 1 < len(tiles) else None
        old_peak = peak_ref[rows, :]
        peak = jnp.maximum(old_peak, jnp.max(scores, axis=1, keepdims=True))
        factor = jnp.exp2((old_peak - peak) * EXP_SCALE)
        peaks = jnp.concatenate([peak] * (keys.size // HEAD), axis=1)
        weights = jnp.exp2((scores - peaks) * EXP_SCALE).astype(jnp.bfloat16)
        added = jnp.dot(weights, value_of(keys), preferred_element_type=jnp.float32)
        acc_ref[rows, :] = acc_ref[rows, :] * widened(factor, factor) + added
        peak_ref[rows, :] = peak
        scores = following


def kernel(
    q_hbm, k_hbm, v_hbm, len_ref, group_ref, pos_ref, out_ref,
    q_ref, k_ref, v_ref, q_send, q_low, q_high,
    kv_send, kv_recv_0, kv_recv_1, kv_all, key_doc, query_doc, queries,
    rank_send, rank_recv, rank_smem, doc_own, doc_recv,
    peak, acc, result_low, result_high, back_send_low, back_send_high, back_recv,
    in_sem, q_ssem, q_rsem, m_ssem, m_rsem, kv_ssem, kv_rsem,
    ring_ssem, ring_rsem, core_ssem, core_rsem, doc_ssem, doc_rsem,
    back_ssem, back_rsem, local_sem, t_ssem, t_rsem,
):
    dp = lax.axis_index("dp")
    ctx = lax.axis_index("ctx")
    z_lo, x, core = dp // 8, (dp // 2) % 4, dp % 2
    z_hi, y = ctx // RING, ctx % RING
    my_seq = z_lo * 8 + x * 2 + z_hi
    own_seg = core * RING + y
    stays = core == z_hi
    kv_recv = (kv_recv_0, kv_recv_1)
    q_recv = (q_low, q_high)
    result = (result_low, result_high)
    back_send = (back_send_low, back_send_high)

    def device(z_lo_, x_, core_, z_hi_, y_):
        return (z_lo_ * 8 + x_ * 2 + core_, z_hi_ * RING + y_)

    up = device(z_lo, x, core, z_hi, (y + 1) % RING)
    down = device(z_lo, x, core, z_hi, (y + 3) % RING)
    twin = device(z_lo, x, 1 - core, z_hi, y)

    def remote(src, dst, ssem, rsem, target):
        return pltpu.make_async_remote_copy(
            src_ref=src, dst_ref=dst, send_sem=ssem, recv_sem=rsem,
            device_id=target, device_id_type=MESH,
        )

    def await_bytes(ref, sem):
        pltpu.make_async_copy(ref, ref, sem).wait()

    loads = [
        pltpu.make_async_copy(src, dst, in_sem.at[at])
        for at, (src, dst) in enumerate(((q_hbm, q_ref), (k_hbm, k_ref), (v_hbm, v_ref)))
    ]
    for load in loads:
        load.start()

    barrier = pltpu.get_barrier_semaphore()
    for at in range(1, 32):
        peer = device(
            (z_lo + at % 2) % 2, (x + (at // 2) % 4) % 4, (core + (at // 8) % 2) % 2, (z_hi + at // 16) % 2, y
        )
        pl.semaphore_signal(barrier, inc=1, device_id=peer, device_id_type=MESH)
    for neighbour in (up, down):
        pl.semaphore_signal(barrier, inc=1, device_id=neighbour, device_id_type=MESH)

    lane = lax.broadcasted_iota(jnp.int32, (1, HEAD), 1)
    begin = jnp.zeros((1, HEAD), jnp.int32)
    until = jnp.full((1, HEAD), 1 << 20, jnp.int32)
    total = jnp.int32(0)
    for document in range(4):
        begin = jnp.where(lane == document, total, begin)
        total = total + len_ref[0, document]
        until = jnp.where(lane == document, total, until)
    doc_own[0] = begin
    doc_own[1] = until

    def arrival(seq):
        slot, rank = jnp.int32(0), jnp.int32(-1)
        for block in range(NB):
            hit = group_ref[block] == seq
            slot = jnp.where(hit, block, slot)
            rank = jnp.where(hit, pos_ref[block] % NB, rank)
        return slot, rank

    def offsets_of(at):
        z_step = (3 - at // 4 + at % 4) % 4
        return (2 + 3 * (at % 4)) % 4, z_step % 2, z_step // 2

    def target_of(at):
        x_step, z_step, other = offsets_of(at)
        return (z_lo + z_step) % 2, (x + x_step) % 4, (z_hi + other) % 2

    for load in loads:
        load.wait()

    def stage(at, unused):
        z_lo_, x_, seq_core = target_of(at)
        slot, rank = arrival(z_lo_ * 8 + x_ * 2 + seq_core)
        rank_send[at] = jnp.full((1, HEAD), rank, jnp.int32)
        block = q_ref[slot]
        q_send[at, 0] = block[:HALF]
        q_send[at, 1] = block[HALF:]
        keys, values = k_ref[slot], v_ref[slot]
        for part in range(PARTS):
            kv_send[part, at, 0] = keys[part * PIECE:(part + 1) * PIECE]
            kv_send[part, at, 1] = values[part * PIECE:(part + 1) * PIECE]
        return unused

    lax.fori_loop(0, GROUPS, stage, 0)
    pl.semaphore_wait(barrier, 33)

    remote(doc_own, doc_recv, doc_ssem, doc_rsem, twin).start()

    def to_or_here(here, src, dst, ssem, rsem, target):
        @pl.when(here)
        def _():
            pltpu.make_async_copy(src, dst, rsem).start()

        @pl.when(jnp.logical_not(here))
        def _():
            remote(src, dst, ssem, rsem, target).start()

    def send_ranks():
        def send(at, unused):
            z_lo_, x_, seq_core = target_of(at)
            to_or_here(
                (at == SELF) & stays, rank_send.at[at], rank_recv.at[z_hi, dp], m_ssem, m_rsem,
                device(z_lo_, x_, z_hi, seq_core, y),
            )
            return unused

        lax.fori_loop(0, GROUPS, send, 0)

    def send_queries(plane):
        def send(at, unused):
            z_lo_, x_, seq_core = target_of(at)
            for other in range(2):
                rows = (core + other) % 2
                to_or_here(
                    at + other * GROUPS == SELF, q_send.at[at, rows], q_recv[plane].at[dp],
                    q_ssem, q_rsem.at[plane], device(z_lo_, x_, rows, seq_core, y),
                )
            return unused

        lax.fori_loop(0, GROUPS, send, 0)

    def queries_sent():
        await_bytes(q_send.at[pl.ds(0, GROUPS - 1)], q_ssem)
        await_bytes(q_send.at[0, 0], q_ssem)

    def send_keys(part):
        def send(at, unused):
            z_lo_, x_, seq_core = target_of(at)
            to_or_here(
                (at == SELF) & stays, kv_send.at[part, at], kv_recv[part].at[dp],
                kv_ssem.at[part], kv_rsem.at[part], device(z_lo_, x_, z_hi, seq_core, y),
            )
            return unused

        lax.fori_loop(0, GROUPS, send, 0)

    def keys_sent(part):
        @pl.when(stays)
        def _():
            await_bytes(kv_send.at[part, pl.ds(0, GROUPS - 1)], kv_ssem.at[part])

        @pl.when(jnp.logical_not(stays))
        def _():
            await_bytes(kv_send.at[part], kv_ssem.at[part])

    def issue(batch):
        @pl.when(z_hi == 0)
        def _():
            send_queries(0) if batch == 1 else send_keys(batch // 2)

        @pl.when(z_hi == 1)
        def _():
            send_queries(1) if batch == 0 else send_keys(batch - 1)

    def sent(batch):
        @pl.when(z_hi == 0)
        def _():
            queries_sent() if batch == 1 else keys_sent(batch // 2)

        @pl.when(z_hi == 1)
        def _():
            queries_sent() if batch == 0 else keys_sent(batch - 1)

    send_ranks()
    issue(0)

    remote(doc_own, doc_recv, doc_ssem, doc_rsem, twin).wait()
    begin = jnp.where(stays, doc_own[0], doc_recv[0])
    until = jnp.where(stays, doc_own[1], doc_recv[1])

    def places(first, size):
        return lax.broadcasted_iota(jnp.int32, (size, HEAD), 0) + first

    def key_mark(first, size):
        place = places(first, size)
        return jnp.where((place >= begin) & (place < until), 0.0, FAR).astype(jnp.bfloat16)

    def mark_keys(block, unused):
        rows = pl.ds(pl.multiple_of((block % NB) * PIECE, PIECE), PIECE)
        for part in range(PARTS):
            key_doc[part, block // NB, rows, :] = key_mark(block * BLK + part * PIECE, PIECE)
        return unused

    lax.fori_loop(0, 2 * RING * NB, mark_keys, 0)

    def query_seg(group):
        return y + group * RING

    def prepare(rank, unused):
        rows = pl.ds(pl.multiple_of(rank * HALF, HALF), HALF)
        lanes = lax.broadcasted_iota(jnp.int32, (HALF, HEAD), 1)
        for group in range(2):
            place = places(query_seg(group) * SEG + rank * BLK + core * HALF, HALF)
            inside = (place >= begin) & (place < until) & (lanes < 4)
            query_doc[group, rows, :] = jnp.where(inside, 1.0, 0.0).astype(jnp.bfloat16)
            peak[group, rows, :] = jnp.full((HALF, HEAD), EMPTY, jnp.float32)
            acc[group, rows, :] = jnp.zeros((HALF, 2 * HEAD), jnp.float32)
        return unused

    lax.fori_loop(0, NB, prepare, 0)

    await_bytes(rank_recv.at[core], m_rsem)
    shared = remote(rank_recv.at[core], rank_recv.at[core], t_ssem, t_rsem, twin)
    shared.start()
    shared.wait_send()
    await_bytes(rank_recv.at[1 - core], t_rsem)
    ranks_in = pltpu.make_async_copy(rank_recv, rank_smem, local_sem)
    ranks_in.start()
    ranks_in.wait()

    def source_of(plane, rank):
        source = jnp.int32(0)
        for sender in range(GROUPS):
            source = jnp.where(rank_smem[plane, sender, 0, 0] == rank, sender, source)
        return source

    def take_queries(group):
        await_bytes(q_recv[group], q_rsem.at[group])

        def place(rank, unused):
            rows = pl.ds(pl.multiple_of(rank * HALF, HALF), HALF)
            queries[group, rows, :] = q_recv[group][source_of(group, rank)]
            return unused

        lax.fori_loop(0, NB, place, 0)

    def seg_at(kind, shift):
        return kind * RING + (y + shift) % RING

    def kv_at(part, seg):
        return kv_all.at[part, seg]

    def ring_copy(part, which):
        here = (
            kv_at(part, own_seg), kv_at(part, own_seg),
            kv_at(part, seg_at(core, 3)).at[0], kv_at(part, seg_at(core, 1)).at[1],
        )[which]
        return remote(here, here, ring_ssem.at[part, which], ring_rsem.at[part, which], (up, down)[which % 2])

    def ring_arrived(part, which):
        there = (
            kv_at(part, seg_at(core, 3)), kv_at(part, seg_at(core, 1)),
            kv_at(part, seg_at(core, 2)).at[0], kv_at(part, seg_at(core, 2)).at[1],
        )[which]
        await_bytes(there, ring_rsem.at[part, which])

    def shift_of(step):
        return (0, 3, 1, 2)[step]

    def core_copy(part, step):
        here = kv_at(part, seg_at(core, shift_of(step)))
        return remote(here, here, core_ssem.at[part, step], core_rsem.at[part, step], twin)

    def begin_part(part):
        await_bytes(kv_recv[part], kv_rsem.at[part])

        def place(rank, unused):
            rows = pl.ds(pl.multiple_of(rank * PIECE, PIECE), PIECE)
            source = source_of(core, rank)
            for which in range(2):
                kv_all[part, own_seg, which, rows, :] = kv_recv[part][source, which]
            return unused

        lax.fori_loop(0, NB, place, 0)
        ring_copy(part, 0).start()
        ring_copy(part, 1).start()
        core_copy(part, 0).start()

    def pass_on(part):
        ring_arrived(part, 0)
        ring_copy(part, 2).start()
        core_copy(part, 1).start()
        ring_arrived(part, 1)
        ring_copy(part, 3).start()
        core_copy(part, 2).start()

    def complete(part):
        ring_arrived(part, 2)
        ring_arrived(part, 3)
        core_copy(part, 3).start()

    def unit(part, seg, group, tiles, masked):
        def mask_of(rows, keys):
            row = lax.broadcasted_iota(jnp.int32, (rows.size, 1), 0) + rows.start
            key = lax.broadcasted_iota(jnp.int32, (1, keys.size), 1) + keys.start
            query_place = (row // HALF) * BLK + core * HALF + row % HALF
            return (key // PIECE) * BLK + part * PIECE + key % PIECE <= query_place

        attend_tiles(
            tiles,
            lambda rows: widened(queries[group, rows, :], query_doc[group, rows, :]),
            lambda keys: widened(kv_all[part, seg, 0, keys, :], key_doc[part, seg, keys, :]),
            lambda keys: widened(kv_all[part, seg, 1, keys, :], jnp.ones((keys.size, HEAD), jnp.bfloat16)),
            mask_of if masked else None,
            peak.at[group],
            acc.at[group],
        )

    def finish(group):
        def divide(rank, unused):
            both = acc[group, pl.ds(pl.multiple_of(rank * HALF, HALF), HALF), :]
            result[group][rank] = (both[:, :HEAD] / both[:, HEAD:]).astype(jnp.bfloat16)
            return unused

        lax.fori_loop(0, NB, divide, 0)

        def send(at, unused):
            x_step, z_step, other = offsets_of(at)
            z_lo_, x_, core_ = (z_lo + z_step) % 2, (x + x_step) % 4, (core + other) % 2
            rank = jnp.maximum(rank_smem[group, z_lo_ * 8 + x_ * 2 + core_, 0, 0], 0)
            back_send[group][at] = result[group][rank]
            to_or_here(
                (at == SELF) & (z_hi == group), back_send[group].at[at], back_recv.at[my_seq, core],
                back_ssem.at[group], back_rsem, device(z_lo_, x_, core_, group, y),
            )
            return unused

        lax.fori_loop(0, GROUPS, send, 0)

    def visits_of(part, kind, group, fresh, *steps):
        return [(part, kind, step, group, fresh) for step in steps]

    visits = (
        *visits_of(0, 0, 1, 1, 0, 1, 2, 3),
        *visits_of(0, 0, 0, 0, 0, 1, 2, 3),
        *visits_of(0, 1, 1, 1, 0, 1, 2, 3),
        *visits_of(1, 0, 1, 1, 0),
        *visits_of(1, 0, 0, 0, 0),
        *visits_of(1, 1, 1, 1, 0),
        *visits_of(1, 0, 1, 1, 1, 2),
        *visits_of(1, 0, 0, 0, 1, 2),
        *visits_of(1, 1, 1, 1, 1, 2),
        *visits_of(1, 0, 0, 1, 3),
        *visits_of(1, 0, 1, 0, 3),
        *visits_of(1, 1, 1, 1, 3),
    )

    def go_on(batch):
        sent(batch - 1)
        issue(batch)

    def on(known, act, part):
        return (known, lambda: act(part))

    actions = {
        1: (on(0, pass_on, 0),),
        2: (on(None, go_on, 2), on(1, begin_part, 0)),
        3: (on(0, complete, 0),),
        4: (on(None, take_queries, 0),),
        7: (on(1, pass_on, 0),),
        10: (on(1, complete, 0), on(None, begin_part, 1)),
        15: (on(None, pass_on, 1),),
        21: (on(None, complete, 1),),
        22: (on(None, finish, 0),),
    }
    low, high, whole = pl.ds(0, UNIT // 2), pl.ds(UNIT // 2, UNIT // 2), pl.ds(0, WIDTH)
    half = pl.ds(0, WIDTH // 2)

    def pick(at, values):
        found = jnp.int32(values[0])
        for index in range(1, len(values)):
            found = jnp.where(at == index, values[index], found)
        return found

    def visit(at, unused):
        code = pick(at, [(((part * 2 + kind) * RING + step) * 2 + group) * 2 + fresh for part, kind, step, group, fresh in visits])
        part, kind, step, group, fresh = code // 32, (code // 16) % 2, (code // 4) % 4, (code // 2) % 2, code % 2
        for due, listed in actions.items():
            for core_known, act in listed:
                pl.when(at == due if core_known is None else (at == due) & (core == core_known))(act)

        seg = kind * RING + (y + pick(step, (0, 3, 1, 2))) % RING

        @pl.when((fresh == 1) & (kind != core))
        def _():
            await_bytes(kv_all.at[part, seg], core_rsem.at[part, step])

        wanted = query_seg(group)

        @pl.when(seg < wanted)
        def _():
            unit(part, seg, group, [(low, whole), (high, whole)], False)

        @pl.when(seg == wanted)
        def _():
            unit(part, seg, group, [(pl.ds(UNIT // 4 * n, UNIT // 4), pl.ds(0, WIDTH // 4 * (n + 1))) for n in range(4)], True)

        return unused

    sent(0)
    issue(1)

    @pl.when(core == 0)
    def _():
        begin_part(0)

    take_queries(1)
    lax.fori_loop(0, len(visits), visit, 0)
    finish(1)

    await_bytes(back_recv, back_rsem)

    def put(at, unused):
        seq = group_ref[at]
        out_ref[at, pl.ds(0, HALF), :] = back_recv[seq, 0]
        out_ref[at, pl.ds(HALF, HALF), :] = back_recv[seq, 1]
        return unused

    lax.fori_loop(0, NB, put, 0)

    @pl.when(stays)
    def _():
        await_bytes(rank_recv.at[0, pl.ds(0, GROUPS - 1)], m_ssem)

    @pl.when(jnp.logical_not(stays))
    def _():
        await_bytes(rank_recv.at[0], m_ssem)

    for group in range(2):
        @pl.when(z_hi == group)
        def _():
            await_bytes(back_send[group].at[pl.ds(0, GROUPS - 1)], back_ssem.at[group])

        @pl.when(z_hi != group)
        def _():
            await_bytes(back_send[group], back_ssem.at[group])

    sent(2)
    for part in range(PARTS):
        for which in range(4):
            ring_copy(part, which).wait_send()
            core_copy(part, which).wait_send()


def shards(query_rows, key_rows, value_rows, doc_lens, dest_group, block_pos):
    bf16, i32, f32 = jnp.bfloat16, jnp.int32, jnp.float32
    vmem = pl.BlockSpec(memory_space=pltpu.VMEM)
    smem = pl.BlockSpec(memory_space=pltpu.SMEM)
    anywhere = pl.BlockSpec(memory_space=pl.ANY)
    dma = pltpu.SemaphoreType.DMA
    blocks = (NB, BLK, HEAD)
    slots = (GROUPS, 2, PIECE, HEAD)
    out = pl.pallas_call(
        kernel,
        out_shape=jax.ShapeDtypeStruct(blocks, bf16),
        in_specs=[anywhere, anywhere, anywhere, smem, smem, smem],
        out_specs=vmem,
        scratch_shapes=[
            pltpu.VMEM(blocks, bf16),
            pltpu.VMEM(blocks, bf16),
            pltpu.VMEM(blocks, bf16),
            pltpu.VMEM((GROUPS, 2, HALF, HEAD), bf16),
            pltpu.VMEM((GROUPS, HALF, HEAD), bf16),
            pltpu.VMEM((GROUPS, HALF, HEAD), bf16),
            pltpu.VMEM((PARTS, *slots), bf16),
            *[pltpu.VMEM(slots, bf16) for _ in range(PARTS)],
            pltpu.VMEM((PARTS, 2 * RING, 2, WIDTH, HEAD), bf16),
            pltpu.VMEM((PARTS, 2 * RING, WIDTH, HEAD), bf16),
            pltpu.VMEM((2, UNIT, HEAD), bf16),
            pltpu.VMEM((2, UNIT, HEAD), bf16),
            pltpu.VMEM((GROUPS, 1, HEAD), i32),
            pltpu.VMEM((2, GROUPS, 1, HEAD), i32),
            pltpu.SMEM((2, GROUPS, 1, HEAD), i32),
            pltpu.VMEM((2, 1, HEAD), i32),
            pltpu.VMEM((2, 1, HEAD), i32),
            pltpu.VMEM((2, UNIT, HEAD), f32),
            pltpu.VMEM((2, UNIT, 2 * HEAD), f32),
            pltpu.VMEM((NB, HALF, HEAD), bf16),
            pltpu.VMEM((NB, HALF, HEAD), bf16),
            pltpu.VMEM((GROUPS, HALF, HEAD), bf16),
            pltpu.VMEM((GROUPS, HALF, HEAD), bf16),
            pltpu.VMEM((GROUPS, 2, HALF, HEAD), bf16),
            dma((3,)), dma, dma((2,)), dma, dma, dma((PARTS,)), dma((PARTS,)),
            dma((PARTS, 4)), dma((PARTS, 4)), dma((PARTS, 4)), dma((PARTS, 4)),
            dma, dma, dma((2,)), dma, dma, dma, dma,
        ],
        compiler_params=pltpu.CompilerParams(
            collective_id=0, has_side_effects=True, vmem_limit_bytes=52 * 2**20
        ),
        name="packed_attention",
    )(
        query_rows.reshape(blocks), key_rows.reshape(blocks), value_rows.reshape(blocks),
        doc_lens, dest_group, block_pos,
    )
    return out.reshape(NB * BLK, HEAD)


def solution(mesh):
    both = P(("dp", "ctx"))
    rows = P(("dp", "ctx"), None)
    return jax.shard_map(
        shards,
        mesh=mesh,
        in_specs=(rows, rows, rows, P("dp", None), both, both),
        out_specs=rows,
        check_vma=False,
    )
```
